256 devices in a mesh: seq: 32 (over y_hi, z, core), tensor: 8 (over y_lo, x).
Axes of the slice: x: 4, y: 4 (y_hi: 2, y_lo: 2; y = y_hi * 2 + y_lo), z: 8, core: 2. Of those that a mesh axis runs over, the one named last changes fastest.
Arguments:
- tokens: bfloat16 [2, 4096, 3072], P(None, 'seq'), as said below
- w_query: bfloat16 [3072, 3072], P(None, 'tensor'), as said below
- w_key: bfloat16 [3072, 3072], P(None, 'tensor'), as said below
- w_value: bfloat16 [3072, 3072], P(None, 'tensor'), as said below
- w_out: bfloat16 [3072, 3072], P('tensor'), as said below
- cotangent: bfloat16 [2, 4096, 3072], P(None, 'seq'), may hold values from -6 to 6
- noise_value: float32 [3072, 3072], P('seq', 'tensor'), may hold values from -6 to 6
- noise_out: float32 [3072, 3072], P('tensor', 'seq'), may hold values from -6 to 6
Outputs:
- grad_value: float32 [3072, 3072], P('seq', 'tensor')
- grad_out: float32 [3072, 3072], P('tensor', 'seq')
The draws below stay inside these ranges and needn't reach their ends.
Inputs may be any that keep to these rules, and one draw needn't show every extreme that they name: `tokens`: patch activations. `w_query`: scaled by the fan-in. `w_key`: scaled by the fan-in. `w_value`: scaled by the fan-in. `w_out`: scaled by the fan-in.
All inputs are finite; a program needn't handle non-finite values.
Results may differ from the reference program's by a relative error of at most 0.023.
Values may be sent and summed in bfloat16 or wider, within the bound.
No kernel may reach another device: no remote copies, remote signals or barrier semaphores. Data moves between devices by JAX's collectives and lax.ppermute only.
A program may use at most 128 MiB of HBM per device.

```python
import math
import jax
import jax.numpy as jnp
from jax import lax

D = 3072
HEADS = 24
HEAD_DIM = 128
IMGS = 2
PATCH_DEV = 128
PATCHES = 4096
N_SEQ = 32


def shared_query(key):
    return jax.random.normal(key, (D, HEADS * HEAD_DIM), jnp.float32)


def head_scales(key, repeat):
    rising = 1.0 + 2.0 * jnp.arange(HEADS, dtype=jnp.float32) / HEADS
    rough = jnp.exp(jax.random.uniform(key, (HEADS,), jnp.float32, 0.0, math.log(2.0)))
    return jnp.repeat(rising * rough, repeat) / 2.2


def draw_tokens(key, part):
    key = jax.random.fold_in(key, 11)
    key_one, key_two = jax.random.split(key, 2)
    rising = 1.0 + 2.0 * jnp.arange(D, dtype=jnp.float32) / D
    feature = rising * jnp.exp(jax.random.uniform(key_one, (D,), jnp.float32, 0.0, math.log(4.0))) / 5.0
    normal_base = jnp.clip(jax.random.normal(key_two, (IMGS, PATCHES, D), jnp.float32), -6.0, 6.0)
    values = normal_base * feature
    return values.astype(jnp.bfloat16)


def draw_w_query(key, part):
    shared = shared_query(key)
    return (jnp.clip(shared, -5.0, 5.0) / math.sqrt(D)).astype(jnp.bfloat16)


def draw_w_key(key, part):
    key = jax.random.fold_in(key, 13)
    fresh_part = jax.random.normal(key, (D, HEADS * HEAD_DIM), jnp.float32)
    blended = fresh_part
    return (jnp.clip(blended, -5.0, 5.0) / math.sqrt(D)).astype(jnp.bfloat16)


def draw_w_value(key, part):
    key = jax.random.fold_in(key, 14)
    key_one, key_two = jax.random.split(key)
    columns = head_scales(key_one, HEAD_DIM)
    normal_base = jnp.clip(jax.random.normal(key_two, (D, HEADS * HEAD_DIM), jnp.float32), -5.0, 5.0)
    return (normal_base * columns[None, :] / math.sqrt(D)).astype(jnp.bfloat16)


def draw_w_out(key, part):
    key = jax.random.fold_in(key, 15)
    key_one, key_two = jax.random.split(key)
    row_scale = head_scales(key_one, HEAD_DIM)
    normal_base = jnp.clip(jax.random.normal(key_two, (HEADS * HEAD_DIM, D), jnp.float32), -5.0, 5.0)
    return (normal_base * row_scale[:, None] / math.sqrt(HEADS * HEAD_DIM)).astype(jnp.bfloat16)


def levels(key, dims, shards, low, top_value):
    loudness, own = 1.0, jax.random.fold_in(key, 6)
    for axis_at, blocks in shards:
        steps = jnp.exp(jax.random.uniform(jax.random.fold_in(own, axis_at), (blocks,), jnp.float32, low / len(shards), top_value / len(shards)))
        loudness = loudness * jnp.repeat(steps, dims[axis_at] // blocks).reshape([-1 if axis == axis_at else 1 for axis in range(len(dims))])
    return loudness


def centred(own_key, shape, spread, bound, shards=(), held_as=jnp.bfloat16):
    entries = jax.random.normal(own_key, shape, jnp.float32) * spread
    if len(shards) > 0:
        entries = levels(own_key, shape, shards, -0.22, 0.18) * entries
    return jnp.clip(entries, min=-bound, max=bound).astype(held_as)


def setup_inputs(seed: int = 0) -> dict:
    key_of = jax.random.split(jax.random.key(seed), 9)
    tokens = draw_tokens(jax.random.fold_in(key_of[8], 71), 0)
    w_query = draw_w_query(jax.random.fold_in(key_of[8], 71), 0)
    w_key = draw_w_key(jax.random.fold_in(key_of[8], 71), 0)
    w_value = draw_w_value(jax.random.fold_in(key_of[8], 71), 0)
    w_out = draw_w_out(jax.random.fold_in(key_of[8], 71), 0)
    cotangent = centred(key_of[5], (IMGS, PATCHES, D), 1.0, 6.0, ((1, 32),))
    noise_value = centred(key_of[6], (D, HEADS * HEAD_DIM), 1.0, 6.0, ((0, 32), (1, 8)), jnp.float32)
    noise_out = centred(key_of[7], (HEADS * HEAD_DIM, D), 1.0, 6.0, ((0, 8), (1, 32)), jnp.float32)
    return {"tokens": tokens, "w_query": w_query, "w_key": w_key, "w_value": w_value, "w_out": w_out, "cotangent": cotangent, "noise_value": noise_value, "noise_out": noise_out}


def project_rows(tokens, weight):
    flat_tokens = tokens.reshape(-1, tokens.shape[-1])
    return jnp.dot(flat_tokens, weight, preferred_element_type=jnp.float32).astype(jnp.bfloat16)

def block_product(left_side, right_side):
    left_blocks = left_side.reshape(N_SEQ, PATCH_DEV, left_side.shape[-1])
    right_blocks = right_side.reshape(N_SEQ, PATCH_DEV, right_side.shape[-1])

    def add_block(running, block_pair):
        product = jnp.dot(block_pair[0].T, block_pair[1], preferred_element_type=jnp.float32)
        rounded = lax.optimization_barrier(product.astype(jnp.bfloat16))
        return (running + rounded.astype(jnp.float32), None)
    initial = jnp.zeros((left_side.shape[-1], right_side.shape[-1]), jnp.float32)
    return lax.scan(add_block, initial, (left_blocks, right_blocks))[0]

def heads_first(array):
    return array.reshape(IMGS, PATCHES, HEADS, HEAD_DIM).transpose(0, 2, 1, 3).reshape(IMGS * HEADS, PATCHES, HEAD_DIM)

def heads_last(array):
    return array.reshape(IMGS, HEADS, PATCHES, HEAD_DIM).transpose(0, 2, 1, 3).reshape(IMGS, PATCHES, HEADS * HEAD_DIM)

def reference(tokens, w_query, w_key, w_value, w_out, cotangent, noise_value, noise_out):
    score_scale = 1.0 / math.sqrt(HEAD_DIM)
    queries = heads_first(project_rows(tokens, w_query))
    keys_full = heads_first(project_rows(tokens, w_key))
    values_full = heads_first(project_rows(tokens, w_value))
    d_attn = jnp.dot(cotangent.reshape(-1, D), w_out.T, preferred_element_type=jnp.float32).astype(jnp.bfloat16)
    d_attn = heads_first(d_attn)

    def per_head(head_items):
        query_head, key_head, value_head, grad_head = head_items
        scores = jnp.dot(query_head, key_head.T, preferred_element_type=jnp.float32) * score_scale
        row_totals = jax.nn.logsumexp(scores, axis=1, keepdims=True)
        attn_probs = jnp.exp(scores - row_totals).astype(jnp.bfloat16)
        attended = jnp.dot(attn_probs, value_head, preferred_element_type=jnp.float32).astype(jnp.bfloat16)
        d_value = block_product(attn_probs, grad_head).astype(jnp.bfloat16)
        return (attended, d_value)
    attended, d_value = lax.map(per_head, (queries, keys_full, values_full, d_attn))
    attended = heads_last(attended)
    d_value = heads_last(d_value)
    per_value = []
    per_out = []
    for image_index in range(IMGS):
        per_value.append(block_product(tokens[image_index], d_value[image_index]))
        per_out.append(block_product(attended[image_index], cotangent[image_index]))
    clip_bound = math.sqrt(2.0 * D * HEADS * HEAD_DIM)
    grad_value = noise_value
    grad_out = noise_out
    for image_index in range(IMGS):
        squares = jnp.sum(jnp.square(per_value[image_index])) + jnp.sum(jnp.square(per_out[image_index]))
        factor = clip_bound / (jnp.sqrt(squares) + 0.01)
        grad_value = grad_value + factor * per_value[image_index]
        grad_out = grad_out + factor * per_out[image_index]
    return (grad_value / IMGS, grad_out / IMGS)
```

```python
import functools
import math

import jax
import jax.numpy as jnp
from jax import lax
from jax.experimental import pallas as pl
from jax.experimental.pallas import tpu as pltpu
from jax.sharding import Mesh, PartitionSpec as P

D = 3072
HEADS = 24
HEAD_DIM = 128
F32 = jnp.float32
BF16 = jnp.bfloat16
YH, Z, CORE = 2, 8, 2
SCALE = 1.0 / math.sqrt(HEAD_DIM)


def shift(x, axis, size, by):
    return lax.ppermute(x, axis, [(i, (i + by) % size) for i in range(size)])


def swap(x, axis, size, mask=1):
    return lax.ppermute(x, axis, [(i, i ^ mask) for i in range(size)])


def score_block(key_block, query_block):
    return (
        lax.dot_general(
            key_block, query_block, (((1,), (1,)), ((), ())), preferred_element_type=F32
        )
        * SCALE
    )


def stats_kernel(heads, pieces, *refs):
    q_ref, key_refs, out_ref = refs[0], refs[1 : 1 + pieces], refs[1 + pieces]
    rows = []
    for head in range(heads):
        cols = slice(head * HEAD_DIM, (head + 1) * HEAD_DIM)
        query = q_ref[:, cols]
        top = None
        total = None
        for ref in key_refs:
            scores = score_block(ref[:, cols], query)
            block_top = jnp.max(scores, axis=0, keepdims=True)
            if top is None:
                top = block_top
                total = jnp.sum(jnp.exp(scores - top), axis=0, keepdims=True)
            else:
                new_top = jnp.maximum(top, block_top)
                total = total * jnp.exp(top - new_top) + jnp.sum(
                    jnp.exp(scores - new_top), axis=0, keepdims=True
                )
                top = new_top
        rows.append(top + jnp.log(total))
    rows.append(jnp.zeros((8 - heads, rows[0].shape[1]), F32))
    out_ref[...] = jnp.concatenate(rows, axis=0)


def grad_kernel(heads, slots, z_ref, *refs):
    pieces = len(slots)
    q_ref, da_ref, mine_ref, other_ref = refs[:4]
    key_refs = refs[4 : 4 + pieces]
    dv_ref, att_ref = refs[4 + pieces :]
    width = heads * HEAD_DIM
    here = z_ref[0]
    mine, other = mine_ref[...], other_ref[...]
    top = jnp.maximum(mine, other)
    totals = top + jnp.log(jnp.exp(mine - top) + jnp.exp(other - top))
    for head in range(heads):
        cols = slice(head * HEAD_DIM, (head + 1) * HEAD_DIM)
        value_cols = slice(width + head * HEAD_DIM, width + (head + 1) * HEAD_DIM)
        query = q_ref[:, cols]
        d_attn = da_ref[:, cols]
        row_total = totals[head : head + 1, :]
        attended = None
        for ref, (distance, start) in zip(key_refs, slots):
            scores = score_block(ref[:, cols], query)
            probs = jnp.exp(scores - row_total).astype(BF16)
            d_value = jnp.dot(probs, d_attn, preferred_element_type=F32)
            owner = lax.rem(here + (Z - distance), Z)
            dv_ref[owner, start : start + ref.shape[0], cols] = d_value.astype(BF16)
            part = lax.dot_general(
                ref[:, value_cols], probs, (((0,), (0,)), ((), ())), preferred_element_type=F32
            )
            attended = part if attended is None else attended + part
        att_ref[cols, :] = attended.astype(BF16)


def local(tokens, w_query, w_key, w_value, w_out, cotangent, noise_value, noise_out):
    images, rows, width = tokens.shape
    columns = w_query.shape[1]
    heads = columns // HEAD_DIM
    image = lax.axis_index("yh")
    z = lax.axis_index("z")
    core = lax.axis_index("core")
    flat_tokens = tokens.reshape(images * rows, width)
    flat_cotangent = cotangent.reshape(images * rows, width)
    clip_bound = math.sqrt(2.0 * D * HEADS * HEAD_DIM)

    def project(weight):
        return jnp.dot(flat_tokens, weight, preferred_element_type=F32).astype(BF16)

    def pick(array, index):
        return lax.dynamic_index_in_dim(array, index, 0, keepdims=False)

    def image_rows(array):
        partner = swap(pick(array, 1 - image), "yh", YH)
        return jnp.concatenate([pick(array, image), partner], axis=0)

    def core_order(mine, other, axis=0):
        return jnp.where(
            core == 0,
            jnp.concatenate([mine, other], axis=axis),
            jnp.concatenate([other, mine], axis=axis),
        )

    def both_cores(array):
        return core_order(array, swap(array, "core", CORE))

    keys_values = jnp.concatenate([project(w_key), project(w_value)], axis=1)
    chunk = image_rows(keys_values.reshape(images, rows, 2 * columns))
    forward = backward = chunk
    pieces, slots = [chunk], [(0, 0)]
    for step in range(1, 4):
        forward = shift(forward, "z", Z, 1)
        backward = shift(backward, "z", Z, -1)
        pieces += [forward, backward]
        slots += [(step, 0), (Z - step, 0)]
    half = chunk.shape[0] // 2
    pieces += [shift(forward[:half], "z", Z, 1), shift(backward[half:], "z", Z, -1)]
    slots += [(4, 0), (4, half)]

    d_attn = jnp.einsum("rd,cd->rc", flat_cotangent, w_out, preferred_element_type=F32)
    queries_d = jnp.concatenate([project(w_query), d_attn.astype(BF16)], axis=1)
    queries_d = both_cores(image_rows(queries_d.reshape(images, rows, 2 * columns)))
    queries, d_attn = queries_d[:, :columns], queries_d[:, columns:]

    def half_width(array):
        array = image_rows(array).reshape(2 * rows, 2, width // 2)
        mine = lax.dynamic_index_in_dim(array, core, 1, keepdims=False)
        sent = lax.dynamic_index_in_dim(array, 1 - core, 1, keepdims=False)
        return core_order(mine, swap(sent, "core", CORE))

    tokens_half = half_width(tokens)
    cotangent_half = half_width(cotangent)

    chip_rows = queries.shape[0]
    vmem = pl.BlockSpec(memory_space=pltpu.VMEM)
    stats = pl.pallas_call(
        functools.partial(stats_kernel, heads, len(pieces)),
        out_shape=jax.ShapeDtypeStruct((8, chip_rows), F32),
        in_specs=[vmem] * (1 + len(pieces)),
        out_specs=vmem,
        compiler_params=pltpu.CompilerParams(vmem_limit_bytes=48 * 2**20),
        name="stats",
    )(queries, *pieces)
    other_stats = swap(stats, "core", CORE)
    d_value, attended = pl.pallas_call(
        functools.partial(grad_kernel, heads, tuple(slots)),
        out_shape=(
            jax.ShapeDtypeStruct((Z, 2 * rows, columns), BF16),
            jax.ShapeDtypeStruct((columns, chip_rows), BF16),
        ),
        in_specs=[pl.BlockSpec(memory_space=pltpu.SMEM)] + [vmem] * (4 + len(pieces)),
        out_specs=(vmem, vmem),
        compiler_params=pltpu.CompilerParams(vmem_limit_bytes=48 * 2**20),
        name="grads",
    )(z.reshape(1), queries, d_attn, stats, other_stats, *pieces)

    def scatter(array):
        got = lax.all_to_all(array, "z", 0, 0, tiled=True)
        return jnp.sum(got.astype(F32), axis=0)

    d_value = both_cores(scatter(d_value).astype(BF16))
    attended = (
        attended.astype(F32) + swap(attended, "core", CORE).astype(F32)
    ).astype(BF16)

    per_value = lax.dot_general(
        tokens_half, d_value, (((0,), (0,)), ((), ())), preferred_element_type=F32
    ).astype(BF16)
    per_out = lax.dot_general(
        cotangent_half, attended, (((0,), (1,)), ((), ())), preferred_element_type=F32
    ).astype(BF16)
    out_shard = scatter(per_out.reshape(Z, width // 2 // Z, columns))
    value_shard = scatter(per_value.reshape(Z, width // 2 // Z, columns))

    squares = jnp.sum(jnp.square(value_shard)) + jnp.sum(jnp.square(out_shard))
    squares = jnp.full((8, 128), squares, F32)
    for axis, size, mask in (
        ("core", 2, 1), ("z", 8, 1), ("z", 8, 3), ("z", 8, 7), ("yl", 2, 1), ("x", 4, 1), ("x", 4, 3),
    ):
        squares = squares + swap(squares, axis, size, mask)
    other_squares = swap(squares, "yh", YH)

    def to_factor(total):
        return clip_bound / (jnp.sqrt(total[0, 0]) + 0.01)

    shards = jnp.concatenate([value_shard, out_shard], axis=1)
    shards = shards.reshape(2, shards.shape[0] // 2, 2 * columns)
    pairs = ([(0, 0), (1, 2), (2, 1), (3, 3)], [(0, 1), (1, 3), (2, 0), (3, 2)])
    along = [
        [((s // 2 * Z + k) * 2 + s % 2, (t // 2 * Z + k) * 2 + t % 2) for k in range(Z) for s, t in pair]
        for pair in pairs
    ]
    axes = ("yh", "z", "core")
    of_core = lax.ppermute(pick(shards, image), axes, along[0])
    of_other = lax.ppermute(pick(shards, 1 - image), axes, along[1])
    own_factor, other_factor = to_factor(squares), to_factor(other_squares)
    same = core == image
    weighted = (
        jnp.where(same, own_factor, other_factor) * of_core
        + jnp.where(same, other_factor, own_factor) * of_other
    )
    grad_value = (weighted[:, :columns] + noise_value) / images
    grad_out = (weighted[:, columns:].T + noise_out) / images
    return grad_value, grad_out


def solution(mesh):
    fine = Mesh(mesh.devices.reshape(YH, Z, CORE, 2, 4), ("yh", "z", "core", "yl", "x"))
    seq, tensor = ("yh", "z", "core"), ("yl", "x")
    placed = (
        P(None, seq, None),
        P(None, tensor),
        P(None, tensor),
        P(None, tensor),
        P(tensor, None),
        P(None, seq, None),
        P(seq, tensor),
        P(tensor, seq),
    )
    return jax.shard_map(
        local,
        mesh=fine,
        in_specs=placed,
        out_specs=(P(seq, tensor), P(tensor, seq)),
        check_vma=False,
    )
```

```python
import functools
import math

import jax
import jax.numpy as jnp
from jax import lax
from jax.experimental import pallas as pl
from jax.experimental.pallas import tpu as pltpu
from jax.sharding import Mesh, PartitionSpec as P

D = 3072
HEADS = 24
HEAD_DIM = 128
F32 = jnp.float32
BF16 = jnp.bfloat16
YH, Z, CORE = 2, 8, 2
SMALL, LARGE = 24 * 2**20, 60 * 2**20
SCALE = 1.0 / math.sqrt(HEAD_DIM)


def shift(x, axis, size, by):
    return lax.ppermute(x, axis, [(i, (i + by) % size) for i in range(size)])


def swap(x, axis, size, mask=1):
    return lax.ppermute(x, axis, [(i, i ^ mask) for i in range(size)])


def head_cols(head):
    return slice(head * HEAD_DIM, (head + 1) * HEAD_DIM)


def log_add(left, right):
    top = jnp.maximum(left, right)
    return top + jnp.log(jnp.exp(left - top) + jnp.exp(right - top))


class Arriving:
    def __init__(self, source, target, sem):
        self.copy = pltpu.make_async_copy(source, target, sem)
        self.target, self.here = target, False
        self.copy.start()

    def ref(self):
        if not self.here:
            self.copy.wait()
            self.here = True
        return self.target

    def __getitem__(self, at):
        return self.ref()[at]


class Leaving:
    def __init__(self, source, target, sem):
        self.copy = pltpu.make_async_copy(source, target, sem)
        self.ref, self.sent = source, False

    def send(self):
        if not self.sent:
            self.copy.start()
            self.sent = True


def call(body, name, scalars, inputs, outputs, views=None, vmem=SMALL):
    views = views or {}
    n_scalars, n_inputs, n_outputs = len(scalars), len(inputs), len(outputs)
    shapes = [views[at][0] if at in views else x.shape for at, x in enumerate(inputs)]

    def kernel(*refs):
        numbers, refs = refs[:n_scalars], refs[n_scalars:]
        sources, refs = refs[:n_inputs], refs[n_inputs:]
        targets, refs = refs[:n_outputs], refs[n_outputs:]
        in_sems, out_sems = refs[-2:]
        numbers = [ref[0] for ref in numbers]
        arriving = []
        for at, source in enumerate(sources):
            if at in views:
                source = source.at[views[at][1](*numbers)]
            arriving.append(Arriving(source, refs[at], in_sems.at[at]))
        leaving = [
            Leaving(refs[n_inputs + at], target, out_sems.at[at])
            for at, target in enumerate(targets)
        ]
        body(numbers, arriving, leaving)
        for one in arriving:
            one.ref()
        for one in leaving:
            one.send()
        for one in leaving:
            one.copy.wait()

    hbm = pl.BlockSpec(memory_space=pltpu.HBM)
    smem = pl.BlockSpec(memory_space=pltpu.SMEM)
    return pl.pallas_call(
        kernel,
        out_shape=tuple(outputs),
        in_specs=[smem] * n_scalars + [hbm] * n_inputs,
        out_specs=(hbm,) * n_outputs,
        scratch_shapes=[pltpu.VMEM(size, x.dtype) for size, x in zip(shapes, inputs)]
        + [pltpu.VMEM(x.shape, x.dtype) for x in outputs]
        + [pltpu.SemaphoreType.DMA((n_inputs,)), pltpu.SemaphoreType.DMA((n_outputs,))],
        compiler_params=pltpu.CompilerParams(vmem_limit_bytes=vmem),
        cost_estimate=pl.CostEstimate(flops=1000, bytes_accessed=0, transcendentals=0),
        name=name,
    )(*scalars, *inputs)


def score_block(key_block, query_block):
    last = (((1,), (1,)), ((), ()))
    return lax.dot_general(key_block, query_block, last, preferred_element_type=F32) * SCALE


def stats_body(heads, pieces, numbers, arriving, leaving):
    query, keys, carried = arriving[0], arriving[1 : 1 + pieces], arriving[1 + pieces :]
    rows = []
    for head in range(heads):
        cols = head_cols(head)
        blocks = [score_block(key[:, cols], query[:, cols]) for key in keys]
        tops = [jnp.max(scores, axis=0, keepdims=True) for scores in blocks]
        top = functools.reduce(jnp.maximum, tops)
        total = sum(jnp.sum(jnp.exp(scores - top), axis=0, keepdims=True) for scores in blocks)
        rows.append(top + jnp.log(total))
    rows.append(jnp.zeros((8 - heads, rows[0].shape[1]), F32))
    found = jnp.concatenate(rows, axis=0)
    for one in carried:
        found = log_add(found, one[...])
    leaving[0].ref[...] = found


def both_totals(mine, other):
    other = other[...]
    half = other.shape[1] // 2
    other = jnp.concatenate([other[:, half:], other[:, :half]], axis=1)
    return log_add(mine[...], other)


def d_value_body(heads, slots, numbers, arriving, leaving):
    (here,) = numbers
    query, d_attn, mine, other = arriving[:4]
    keys, pieces = arriving[4:], len(slots)
    out, kept = leaving[0], leaving[1:]
    totals = both_totals(mine, other)

    def scores(head, piece):
        cols = head_cols(head)
        return score_block(keys[piece][:, cols], query[:, cols])

    order = [(head, piece) for head in range(heads) for piece in range(pieces)]
    ahead = scores(*order[0])
    for at, (head, piece) in enumerate(order):
        block = ahead
        if at + 1 < len(order):
            ahead = scores(*order[at + 1])
        cols = head_cols(head)
        probs = jnp.exp(block - totals[head : head + 1, :]).astype(BF16)
        kept[piece].ref[head] = probs
        d_value = jnp.dot(probs, d_attn[:, cols], preferred_element_type=F32)
        distance, start = slots[piece]
        owner = lax.rem(here + (Z - distance), Z)
        out.ref[owner, start : start + probs.shape[0], cols] = d_value.astype(BF16)
        if head == heads - 1:
            kept[piece].send()


def attend_body(heads, numbers, arriving, leaving):
    pieces = len(arriving) // 2
    probs, values, (out,) = arriving[:pieces], arriving[pieces:], leaving
    half = out.ref.shape[2]
    first = (((0,), (0,)), ((), ()))
    for head in range(heads):
        cols = head_cols(head)
        attended = jnp.zeros((HEAD_DIM, 2 * half), F32)
        for prob, value in zip(probs, values):
            attended += lax.dot_general(
                value[:, cols], prob[head], first, preferred_element_type=F32
            )
        out.ref[0, cols, :] = attended[:, :half].astype(BF16)
        out.ref[1, cols, :] = attended[:, half:].astype(BF16)


def turn_body(numbers, arriving, leaving):
    core, _ = numbers
    keep, send = leaving
    for at, one in enumerate(arriving):
        array = one[...]
        rows, width = array.shape
        low, high = array[:, : width // 2].T, array[:, width // 2 :].T
        to = slice(at * rows, (at + 1) * rows)
        keep.ref[:, to] = jnp.where(core == 0, low, high)
        send.ref[:, to] = jnp.where(core == 0, high, low)


def value_grad_body(numbers, arriving, leaving):
    (here,) = numbers
    mine, other, dv_mine, dv_other = [one.ref() for one in arriving]
    rows = leaving[0].ref.shape[1]
    for output, part, ahead, start, count in (
        (2, 0, 4, 0, rows // 2),
        (3, 0, 4, rows // 2, rows // 2),
        (0, 0, 1, 0, rows),
        (0, 1, 3, 0, rows),
        (1, 0, 7, 0, rows),
        (1, 1, 5, 0, rows),
        (4, 0, 2, 0, rows),
        (5, 0, 6, 0, rows),
        (6, 0, 0, 0, rows),
    ):
        first = lax.rem(here + ahead, Z) * rows + start
        at = pl.ds(pl.multiple_of(first, rows // 2), count)
        product = jnp.dot(mine[at, :], dv_mine[...], preferred_element_type=F32)
        product += jnp.dot(other[at, :], dv_other[...], preferred_element_type=F32)
        leaving[output].ref[part] = product.astype(BF16)
        if part == leaving[output].ref.shape[0] - 1:
            leaving[output].send()


def out_grad_body(numbers, arriving, leaving):
    mine, other, att, att_other = arriving
    (out,) = leaving
    att_mine = (att[0].astype(F32) + att_other[1].astype(F32)).astype(BF16)
    att_rest = (att[1].astype(F32) + att_other[0].astype(F32)).astype(BF16)
    last = (((1,), (1,)), ((), ()))
    rows = out.ref.shape[0] // Z
    for part in range(Z):
        at = slice(part * rows, (part + 1) * rows)
        product = lax.dot_general(mine[at, :], att_mine, last, preferred_element_type=F32)
        product += lax.dot_general(other[at, :], att_rest, last, preferred_element_type=F32)
        out.ref[at, :] = product.astype(BF16)


def relay_body(numbers, arriving, leaving):
    near_f, near_b, far_f, far_b, keep_f, keep_b = arriving
    half = far_f.ref().shape[1]
    for near, far, keep, send, low in (
        (near_f, far_f, keep_f, leaving[0], 0),
        (near_b, far_b, keep_b, leaving[1], half),
    ):
        at, rest = slice(low, low + half), slice(half - low, 2 * half - low)
        through = near[1, at, :].astype(F32) + far[0].astype(F32)
        send.ref[0, at, :] = (keep[0, at, :].astype(F32) + through).astype(BF16)
        through = near[1, rest, :].astype(F32)
        send.ref[0, rest, :] = (keep[0, rest, :].astype(F32) + through).astype(BF16)
        send.send()


def total_of(own, near_f, near_b, last_f, last_b):
    near = near_f[0].astype(F32) + near_b[0].astype(F32)
    return own[0].astype(F32) + near + (last_f[0].astype(F32) + last_b[0].astype(F32))


def sum_body(numbers, arriving, leaving):
    total = sum(arriving[0][part].astype(F32) for part in range(Z))
    leaving[0].ref[...] = total.astype(BF16)


def shard_body(numbers, arriving, leaving):
    out, *terms = arriving
    shard, square_out = leaving
    columns = shard.ref.shape[1] // 2
    square = jnp.zeros((1, 1), F32)
    for total, at in ((out[...].astype(F32), columns), (total_of(*terms), 0)):
        shard.ref[:, at : at + columns] = total.astype(BF16)
        column_sums = jnp.sum(total * total, axis=0, keepdims=True)
        square += jnp.sum(column_sums, axis=1, keepdims=True)
    square_out.ref[...] = jnp.broadcast_to(square.reshape(1, 1, 1), square_out.ref.shape)


def sum_parts(parts, first, count):
    return functools.reduce(jnp.add, [parts[first + at] for at in range(count)])


def square_body(numbers, arriving, leaving):
    total = sum_parts(arriving[0], 0, Z * CORE)
    leaving[0].ref[...] = jnp.broadcast_to(total[None], leaving[0].ref.shape)


def final_body(numbers, arriving, leaving):
    (core,) = numbers
    squares, near, far, noise_value, noise_out = arriving
    value, out = leaving
    columns = value.ref.shape[1]
    clip_bound = math.sqrt(2.0 * D * HEADS * HEAD_DIM)
    factors = []
    for image in range(YH):
        total = sum_parts(squares, image * 8, 8)[0:1, 0:1]
        factors.append(clip_bound / (jnp.sqrt(total) + 0.01))
    near_factor = jnp.where(core == 0, factors[0], factors[1])
    far_factor = jnp.where(core == 0, factors[1], factors[0])
    weighted = near_factor * near[...].astype(F32) + far_factor * far[...].astype(F32)
    value.ref[...] = (weighted[:, :columns] + noise_value[...]) * 0.5
    out.ref[...] = (weighted[:, columns:].T + noise_out[...]) * 0.5


def local(tokens, w_query, w_key, w_value, w_out, cotangent, noise_value, noise_out):
    images, rows, width = tokens.shape
    columns = w_query.shape[1]
    heads = columns // HEAD_DIM
    image = lax.axis_index("yh")
    z = lax.axis_index("z")
    core = lax.axis_index("core")
    flat_tokens = tokens.reshape(images * rows, width)
    flat_cotangent = cotangent.reshape(images * rows, width)
    shape = jax.ShapeDtypeStruct
    here, this_core, this_image = z.reshape(1), core.reshape(1), image.reshape(1)

    def project(weight):
        return jnp.dot(flat_tokens, weight, preferred_element_type=F32).astype(BF16)

    def pick(array, index):
        return lax.dynamic_index_in_dim(array, index, 0, keepdims=False)

    def image_rows(array):
        array = array.reshape(images, rows, array.shape[1])
        partner = swap(pick(array, 1 - image), "yh", YH)
        return jnp.concatenate([pick(array, image), partner], axis=0)

    def from_partner(array):
        return lax.all_gather(pick(array, 1 - image), "yh", axis=0)

    keys_values = jnp.concatenate([project(w_key), project(w_value)], axis=1)
    cotangent_pair = cotangent, from_partner(cotangent)
    chunk = image_rows(keys_values)
    d_attn = jnp.einsum("rd,cd->rc", flat_cotangent, w_out, preferred_element_type=F32)
    queries_d = jnp.concatenate([project(w_query), d_attn.astype(BF16)], axis=1)
    chunk, queries_d, late_tokens = lax.optimization_barrier((chunk, queries_d, tokens))
    queries_d = image_rows(queries_d)
    tokens_pair = tokens, from_partner(late_tokens)
    queries_d = jnp.concatenate([queries_d, swap(queries_d, "core", CORE)], axis=0)
    chip_rows = queries_d.shape[0]

    def stats_of(chosen, *carried):
        (found,) = call(
            functools.partial(stats_body, heads, len(chosen)),
            "stats",
            (),
            (queries_d, *chosen, *carried),
            (shape((8, chip_rows), F32),),
            {at: left_part(x) for at, x in enumerate((queries_d, *chosen))},
        )
        return found

    def left_part(x):
        return (x.shape[0], columns), lambda *_: (slice(None), slice(0, columns))

    def right_part(x):
        return (x.shape[0], columns), lambda *_: (slice(None), slice(columns, 2 * columns))

    forward = backward = chunk
    pieces = [chunk]
    for step in range(1, 4):
        forward = shift(forward, "z", Z, 1)
        backward = shift(backward, "z", Z, -1)
        pieces += [forward, backward]
        if step == 3:
            stats = stats_of(pieces[:3])
            forward, backward, stats = lax.optimization_barrier((forward, backward, stats))
    half = chunk.shape[0] // 2
    pieces += [shift(forward[:half], "z", Z, 1), shift(backward[half:], "z", Z, -1)]
    stats = stats_of(pieces[3:7], stats)
    stats = stats_of(pieces[7:], stats)
    other_stats = swap(stats, "core", CORE)

    def block(parts, count):
        return shape((parts, count, columns), BF16)

    def start_scatter(near_f, near_b, far_f, far_b):
        return (
            shift(near_f, "z", Z, 1),
            shift(near_b, "z", Z, -1),
            shift(far_f, "z", Z, 2),
            shift(far_b, "z", Z, -2),
        )

    def relay(arrived, keep_f, keep_b):
        like = shape(keep_f.shape, BF16)
        return call(relay_body, "relay", (), (*arrived, keep_f, keep_b), (like, like))

    def end_scatter(arrived, sums, own):
        return own, arrived[0], arrived[1], shift(sums[0], "z", Z, 2), shift(sums[1], "z", Z, -2)

    slots = ((0, 0), (1, 0), (7, 0), (2, 0), (6, 0), (3, 0), (5, 0), (4, 0), (4, half))
    inputs = (queries_d, queries_d, stats, other_stats, *pieces)
    views = {at: left_part(inputs[at]) for at in (0, *range(4, len(inputs)))}
    d_value, *probs = call(
        functools.partial(d_value_body, heads, slots),
        "d_value",
        (here,),
        inputs,
        (block(Z, 2 * rows),) + tuple(shape((heads, x.shape[0], chip_rows), BF16) for x in pieces),
        {**views, 1: right_part(queries_d)},
        LARGE,
    )
    d_value, probs, cotangent_pair = lax.optimization_barrier((d_value, probs, cotangent_pair))
    terms = lax.all_to_all(d_value, "z", 0, 0, tiled=True)
    (attended,) = call(
        functools.partial(attend_body, heads),
        "attend",
        (),
        (*probs, *pieces),
        (shape((2, columns, chip_rows // 2), BF16),),
        {len(pieces) + at: right_part(x) for at, x in enumerate(pieces)},
        LARGE,
    )
    attended_other = swap(attended, "core", CORE)
    attended, tokens_pair = lax.optimization_barrier((attended, tokens_pair))

    def half_width(pair):
        turned = shape((width // 2, 2 * rows), BF16)
        keep, send = call(
            turn_body,
            "turn",
            (this_core, this_image),
            pair,
            (turned, turned),
            {
                0: ((rows, width), lambda core, image: image),
                1: ((rows, width), lambda core, image: 1 - image),
            },
            LARGE,
        )
        return keep, swap(send, "core", CORE)

    cotangent_half = half_width(cotangent_pair)
    tokens_half = half_width(tokens_pair)
    (per_out,) = call(
        out_grad_body,
        "per_out",
        (),
        (*cotangent_half, attended, attended_other),
        (shape((width // 2, columns), BF16),),
        vmem=LARGE,
    )
    out_shard = lax.psum_scatter(per_out, "z", scatter_dimension=0, tiled=True)

    (d_value,) = call(sum_body, "d_value_sum", (), (terms,), (shape((2 * rows, columns), BF16),))
    count = width // 2 // Z
    parts = call(
        value_grad_body,
        "per_value",
        (here,),
        (*tokens_half, d_value, swap(d_value, "core", CORE)),
        (block(2, count), block(2, count), block(1, count // 2), block(1, count // 2)) + (block(1, count),) * 3,
        vmem=LARGE,
    )
    arrived = start_scatter(*parts[:4])
    terms = end_scatter(arrived, relay(arrived, *parts[4:6]), parts[6])
    small = shape((Z * CORE, 8, 128), F32)
    shard, square = call(
        shard_body,
        "shards",
        (),
        (out_shard, *terms),
        (shape((count, 2 * columns), BF16), small),
        vmem=LARGE,
    )

    halves = shard.reshape(2, count // 2, 2 * columns)
    pairs = ([(0, 0), (1, 2), (2, 1), (3, 3)], [(0, 1), (1, 3), (2, 0), (3, 2)])
    along = [
        [((s // 2 * Z + k) * 2 + s % 2, (t // 2 * Z + k) * 2 + t % 2) for k in range(Z) for s, t in pair]
        for pair in pairs
    ]
    axes = ("yh", "z", "core")
    near = lax.ppermute(pick(halves, image), axes, along[0])
    far = lax.ppermute(pick(halves, 1 - image), axes, along[1])

    squares = lax.all_to_all(square, ("z", "core"), 0, 0, tiled=True)
    (squares,) = call(square_body, "squares", (), (squares,), (small,))
    squares = lax.all_to_all(squares, ("yh", "yl", "x"), 0, 0, tiled=True)
    return call(
        final_body,
        "final",
        (this_core,),
        (squares, near, far, noise_value, noise_out),
        (shape(noise_value.shape, F32), shape(noise_out.shape, F32)),
    )


def solution(mesh):
    fine = Mesh(mesh.devices.reshape(YH, Z, CORE, 2, 4), ("yh", "z", "core", "yl", "x"))
    seq, tensor = ("yh", "z", "core"), ("yl", "x")
    placed = (
        P(None, seq, None),
        P(None, tensor),
        P(None, tensor),
        P(None, tensor),
        P(tensor, None),
        P(None, seq, None),
        P(seq, tensor),
        P(tensor, seq),
    )
    return jax.shard_map(
        local,
        mesh=fine,
        in_specs=placed,
        out_specs=(P(seq, tensor), P(tensor, seq)),
        check_vma=False,
    )
```

```python
import functools
import math

import jax
import jax.numpy as jnp
from jax import lax
from jax.experimental import pallas as pl
from jax.experimental.pallas import tpu as pltpu
from jax.sharding import Mesh, PartitionSpec as P

D = 3072
HEADS = 24
HEAD_DIM = 128
F32 = jnp.float32
BF16 = jnp.bfloat16
YH, Z, CORE = 2, 8, 2
SMALL, LARGE = 24 * 2**20, 60 * 2**20
SCALE = 1.0 / math.sqrt(HEAD_DIM)


def shift(x, axis, size, by):
    return lax.ppermute(x, axis, [(i, (i + by) % size) for i in range(size)])


def swap(x, axis, size, mask=1):
    return lax.ppermute(x, axis, [(i, i ^ mask) for i in range(size)])


def head_cols(head):
    return slice(head * HEAD_DIM, (head + 1) * HEAD_DIM)


def log_add(left, right):
    top = jnp.maximum(left, right)
    return top + jnp.log(jnp.exp(left - top) + jnp.exp(right - top))


class Arriving:
    def __init__(self, source, target, sem):
        self.copy = pltpu.make_async_copy(source, target, sem)
        self.target, self.here = target, False
        self.copy.start()

    def ref(self):
        if not self.here:
            self.copy.wait()
            self.here = True
        return self.target

    def __getitem__(self, at):
        return self.ref()[at]


class Leaving:
    def __init__(self, source, target, sem):
        self.copy = pltpu.make_async_copy(source, target, sem)
        self.ref, self.sent = source, False

    def send(self):
        if not self.sent:
            self.copy.start()
            self.sent = True


def call(body, name, scalars, inputs, outputs, views=None, vmem=SMALL):
    views = views or {}
    n_scalars, n_inputs, n_outputs = len(scalars), len(inputs), len(outputs)
    shapes = [views[at][0] if at in views else x.shape for at, x in enumerate(inputs)]

    def kernel(*refs):
        numbers, refs = refs[:n_scalars], refs[n_scalars:]
        sources, refs = refs[:n_inputs], refs[n_inputs:]
        targets, refs = refs[:n_outputs], refs[n_outputs:]
        in_sems, out_sems = refs[-2:]
        numbers = [ref[0] for ref in numbers]
        arriving = []
        for at, source in enumerate(sources):
            if at in views:
                source = source.at[views[at][1](*numbers)]
            arriving.append(source if small[at] else Arriving(source, refs[at], in_sems.at[at]))
        leaving = [
            Leaving(refs[n_inputs + at], target, out_sems.at[at])
            for at, target in enumerate(targets)
        ]
        body(numbers, arriving, leaving)
        for at, one in enumerate(arriving):
            if not small[at]:
                one.ref()
        for one in leaving:
            one.send()
        for one in leaving:
            one.copy.wait()

    hbm = pl.BlockSpec(memory_space=pltpu.HBM)
    smem = pl.BlockSpec(memory_space=pltpu.SMEM)
    in_vmem = pl.BlockSpec(memory_space=pltpu.VMEM)
    small = [x.dtype == F32 and x.size <= 2**15 for x in inputs]
    return pl.pallas_call(
        kernel,
        out_shape=tuple(outputs),
        in_specs=[smem] * n_scalars + [in_vmem if one else hbm for one in small],
        out_specs=(hbm,) * n_outputs,
        scratch_shapes=[pltpu.VMEM(size, x.dtype) for size, x in zip(shapes, inputs)]
        + [pltpu.VMEM(x.shape, x.dtype) for x in outputs]
        + [pltpu.SemaphoreType.DMA((n_inputs,)), pltpu.SemaphoreType.DMA((n_outputs,))],
        compiler_params=pltpu.CompilerParams(vmem_limit_bytes=vmem),
        cost_estimate=pl.CostEstimate(flops=1000, bytes_accessed=0, transcendentals=0),
        name=name,
    )(*scalars, *inputs)


def score_block(key_block, query_block):
    last = (((1,), (1,)), ((), ()))
    return lax.dot_general(key_block, query_block, last, preferred_element_type=F32) * SCALE


def stats_body(heads, pieces, numbers, arriving, leaving):
    query, keys, carried = arriving[0], arriving[1 : 1 + pieces], arriving[1 + pieces :]
    rows = []
    for head in range(heads):
        cols = head_cols(head)
        blocks = [score_block(key[:, cols], query[:, cols]) for key in keys]
        tops = [jnp.max(scores, axis=0, keepdims=True) for scores in blocks]
        top = functools.reduce(jnp.maximum, tops)
        total = sum(jnp.sum(jnp.exp(scores - top), axis=0, keepdims=True) for scores in blocks)
        rows.append(top + jnp.log(total))
    rows.append(jnp.zeros((8 - heads, rows[0].shape[1]), F32))
    found = jnp.concatenate(rows, axis=0)
    for one in carried:
        found = log_add(found, one[...])
    leaving[0].ref[...] = found


def both_totals(mine, other):
    other = other[...]
    half = other.shape[1] // 2
    other = jnp.concatenate([other[:, half:], other[:, :half]], axis=1)
    return log_add(mine[...], other)


def d_value_body(heads, slots, numbers, arriving, leaving):
    (here,) = numbers
    query, d_attn, mine, other = arriving[:4]
    keys, pieces = arriving[4:], len(slots)
    out, att = leaving
    half = att.ref.shape[2]
    totals = both_totals(mine, other)

    def scores(head, piece):
        cols = head_cols(head)
        return score_block(keys[piece][:, cols], query[:, cols])

    order = [(head, piece) for head in range(heads) for piece in range(pieces)]
    ahead = scores(*order[0])
    for at, (head, piece) in enumerate(order):
        block = ahead
        if at + 1 < len(order):
            ahead = scores(*order[at + 1])
        cols = head_cols(head)
        probs = jnp.exp(block - totals[head : head + 1, :]).astype(BF16)
        d_value = jnp.dot(probs, d_attn[:, cols], preferred_element_type=F32)
        distance, start = slots[piece]
        owner = lax.rem(here + (Z - distance), Z)
        out.ref[owner, start : start + probs.shape[0], cols] = d_value.astype(BF16)
        first = (((0,), (0,)), ((), ()))
        value = keys[piece][:, head_cols(heads + head)]
        term = lax.dot_general(value, probs, first, preferred_element_type=F32)
        attended = term if piece == 0 else attended + term
        if piece == pieces - 1:
            att.ref[0, cols, :] = attended[:, :half].astype(BF16)
            att.ref[1, cols, :] = attended[:, half:].astype(BF16)


def turn_body(numbers, arriving, leaving):
    core, _ = numbers
    keep, send = leaving
    for at, one in enumerate(arriving):
        array = one[...]
        rows, width = array.shape
        low, high = array[:, : width // 2].T, array[:, width // 2 :].T
        to = slice(at * rows, (at + 1) * rows)
        keep.ref[:, to] = jnp.where(core == 0, low, high)
        send.ref[:, to] = jnp.where(core == 0, high, low)


def value_grad_body(numbers, arriving, leaving):
    (here,) = numbers
    mine, other, dv_mine, dv_other = [one.ref() for one in arriving]
    rows = leaving[0].ref.shape[1]
    for output, part, ahead, start, count in (
        (2, 0, 4, 0, rows // 2),
        (3, 0, 4, rows // 2, rows // 2),
        (0, 0, 1, 0, rows),
        (0, 1, 3, 0, rows),
        (1, 0, 7, 0, rows),
        (1, 1, 5, 0, rows),
        (4, 0, 2, 0, rows),
        (5, 0, 6, 0, rows),
        (6, 0, 0, 0, rows),
    ):
        first = lax.rem(here + ahead, Z) * rows + start
        at = pl.ds(pl.multiple_of(first, rows // 2), count)
        product = jnp.dot(mine[at, :], dv_mine[...], preferred_element_type=F32)
        product += jnp.dot(other[at, :], dv_other[...], preferred_element_type=F32)
        leaving[output].ref[part] = product.astype(BF16)
        if part == leaving[output].ref.shape[0] - 1:
            leaving[output].send()


def out_grad_body(numbers, arriving, leaving):
    mine, other, att, att_other = arriving
    (out,) = leaving
    att_mine = (att[0].astype(F32) + att_other[1].astype(F32)).astype(BF16)
    att_rest = (att[1].astype(F32) + att_other[0].astype(F32)).astype(BF16)
    last = (((1,), (1,)), ((), ()))
    rows = out.ref.shape[0] // Z
    for part in range(Z):
        at = slice(part * rows, (part + 1) * rows)
        product = lax.dot_general(mine[at, :], att_mine, last, preferred_element_type=F32)
        product += lax.dot_general(other[at, :], att_rest, last, preferred_element_type=F32)
        out.ref[at, :] = product.astype(BF16)


def relay_body(numbers, arriving, leaving):
    near_f, near_b, far_f, far_b, keep_f, keep_b = arriving
    half = far_f.ref().shape[1]
    for near, far, keep, send, low in (
        (near_f, far_f, keep_f, leaving[0], 0),
        (near_b, far_b, keep_b, leaving[1], half),
    ):
        at, rest = slice(low, low + half), slice(half - low, 2 * half - low)
        through = near[1, at, :].astype(F32) + far[0].astype(F32)
        send.ref[0, at, :] = (keep[0, at, :].astype(F32) + through).astype(BF16)
        through = near[1, rest, :].astype(F32)
        send.ref[0, rest, :] = (keep[0, rest, :].astype(F32) + through).astype(BF16)
        send.send()


def total_of(own, near_f, near_b, last_f, last_b):
    near = near_f[0].astype(F32) + near_b[0].astype(F32)
    return own[0].astype(F32) + near + (last_f[0].astype(F32) + last_b[0].astype(F32))


def sum_body(numbers, arriving, leaving):
    total = sum(arriving[0][part].astype(F32) for part in range(Z))
    leaving[0].ref[...] = total.astype(BF16)


def shard_body(numbers, arriving, leaving):
    out, *terms = arriving
    shard, square_out = leaving
    columns = shard.ref.shape[1] // 2
    square = jnp.zeros((1, 1), F32)
    for total, at in ((out[...].astype(F32), columns), (total_of(*terms), 0)):
        shard.ref[:, at : at + columns] = total.astype(BF16)
        column_sums = jnp.sum(total * total, axis=0, keepdims=True)
        square += jnp.sum(column_sums, axis=1, keepdims=True)
    square_out.ref[...] = jnp.broadcast_to(square.reshape(1, 1, 1), square_out.ref.shape)


def sum_parts(parts, first, count):
    return functools.reduce(jnp.add, [parts[first + at] for at in range(count)])


def square_body(numbers, arriving, leaving):
    total = sum_parts(arriving[0], 0, Z * CORE)
    leaving[0].ref[...] = jnp.broadcast_to(total[None], leaving[0].ref.shape)


def final_body(numbers, arriving, leaving):
    (core,) = numbers
    squares, near, far, noise_value, noise_out = arriving
    value, out = leaving
    columns = value.ref.shape[1]
    clip_bound = math.sqrt(2.0 * D * HEADS * HEAD_DIM)
    factors = []
    for image in range(YH):
        total = sum_parts(squares, image * 8, 8)[0:1, 0:1]
        factors.append(clip_bound / (jnp.sqrt(total) + 0.01))
    near_factor = jnp.where(core == 0, factors[0], factors[1])
    far_factor = jnp.where(core == 0, factors[1], factors[0])
    weighted = near_factor * near[...].astype(F32) + far_factor * far[...].astype(F32)
    value.ref[...] = (weighted[:, :columns] + noise_value[...]) * 0.5
    out.ref[...] = (weighted[:, columns:] + noise_out[...]) * 0.5


def local(tokens, w_query, w_key, w_value, w_out, cotangent, noise_value, noise_out):
    images, rows, width = tokens.shape
    columns = w_query.shape[1]
    heads = columns // HEAD_DIM
    image = lax.axis_index("yh")
    z = lax.axis_index("z")
    core = lax.axis_index("core")
    flat_tokens = tokens.reshape(images * rows, width)
    flat_cotangent = cotangent.reshape(images * rows, width)
    shape = jax.ShapeDtypeStruct
    here, this_core, this_image = z.reshape(1), core.reshape(1), image.reshape(1)

    def project(weight):
        return jnp.dot(flat_tokens, weight, preferred_element_type=F32).astype(BF16)

    def pick(array, index):
        return lax.dynamic_index_in_dim(array, index, 0, keepdims=False)

    def image_rows(array):
        array = array.reshape(images, rows, array.shape[1])
        partner = swap(pick(array, 1 - image), "yh", YH)
        return jnp.concatenate([pick(array, image), partner], axis=0)

    def from_partner(array):
        return lax.all_gather(pick(array, 1 - image), "yh", axis=0)

    keys_values = jnp.concatenate([project(w_key), project(w_value)], axis=1)
    chunk = image_rows(keys_values)
    d_attn = jnp.einsum("rd,cd->rc", flat_cotangent, w_out, preferred_element_type=F32)
    queries_d = jnp.concatenate([project(w_query), d_attn.astype(BF16)], axis=1)
    chunk, queries_d = lax.optimization_barrier((chunk, queries_d))
    queries_d = image_rows(queries_d)
    chip_rows = CORE * images * rows

    def stats_of(chosen, *carried):
        (found,) = call(
            functools.partial(stats_body, heads, len(chosen)),
            "stats",
            (),
            (queries_d, *chosen, *carried),
            (shape((8, chip_rows), F32),),
            {at: left_part(x) for at, x in enumerate((queries_d, *chosen))},
        )
        return found

    def left_part(x):
        return (x.shape[0], columns), lambda *_: (slice(None), slice(0, columns))

    def right_part(x):
        return (x.shape[0], columns), lambda *_: (slice(None), slice(columns, 2 * columns))

    forward = backward = chunk
    pieces = [chunk]
    for step in range(1, 4):
        forward = shift(forward, "z", Z, 1)
        backward = shift(backward, "z", Z, -1)
        pieces += [forward, backward]
        if step == 1:
            forward, backward, queries_d, late_tokens, late_cotangent = lax.optimization_barrier(
                (forward, backward, queries_d, tokens, cotangent)
            )
            queries_d = jnp.concatenate([queries_d, swap(queries_d, "core", CORE)], axis=0)
            cotangent_pair = cotangent, from_partner(late_cotangent)
            tokens_pair = tokens, from_partner(late_tokens)
        if step == 3:
            stats = stats_of(pieces[:3])
            forward, backward, stats = lax.optimization_barrier((forward, backward, stats))
    half = chunk.shape[0] // 2
    pieces += [shift(forward[:half], "z", Z, 1), shift(backward[half:], "z", Z, -1)]
    stats = stats_of(pieces[3:7], stats)
    stats = stats_of(pieces[7:], stats)
    other_stats = swap(stats, "core", CORE)

    def block(parts, count):
        return shape((parts, count, columns), BF16)

    def start_scatter(near_f, near_b, far_f, far_b):
        return (
            shift(near_f, "z", Z, 1),
            shift(near_b, "z", Z, -1),
            shift(far_f, "z", Z, 2),
            shift(far_b, "z", Z, -2),
        )

    def relay(arrived, keep_f, keep_b):
        like = shape(keep_f.shape, BF16)
        return call(
            relay_body, "relay", (), (*arrived, keep_f, keep_b), (like, like), vmem=LARGE
        )

    def end_scatter(arrived, sums, own):
        return own, arrived[0], arrived[1], shift(sums[0], "z", Z, 2), shift(sums[1], "z", Z, -2)

    slots = ((0, 0), (1, 0), (7, 0), (2, 0), (6, 0), (3, 0), (5, 0), (4, 0), (4, half))
    d_value, attended = call(
        functools.partial(d_value_body, heads, slots),
        "d_value",
        (here,),
        (queries_d, queries_d, stats, other_stats, *pieces),
        (block(Z, 2 * rows), shape((2, columns, chip_rows // 2), BF16)),
        {0: left_part(queries_d), 1: right_part(queries_d)},
        LARGE,
    )
    attended, cotangent_pair = lax.optimization_barrier((attended, cotangent_pair))
    terms = lax.all_to_all(d_value, "z", 0, 0, tiled=True)
    attended_other = swap(attended, "core", CORE)

    def half_width(pair):
        turned = shape((width // 2, 2 * rows), BF16)
        keep, send = call(
            turn_body,
            "turn",
            (this_core, this_image),
            pair,
            (turned, turned),
            {
                0: ((rows, width), lambda core, image: image),
                1: ((rows, width), lambda core, image: 1 - image),
            },
            LARGE,
        )
        return keep, swap(send, "core", CORE)

    cotangent_half = half_width(cotangent_pair)
    (per_out,) = call(
        out_grad_body,
        "per_out",
        (),
        (*cotangent_half, attended, attended_other),
        (shape((width // 2, columns), BF16),),
        vmem=LARGE,
    )
    per_out, tokens_pair = lax.optimization_barrier((per_out, tokens_pair))
    out_shard = lax.psum_scatter(per_out, "z", scatter_dimension=0, tiled=True)
    tokens_half = half_width(tokens_pair)

    (d_value,) = call(sum_body, "d_value_sum", (), (terms,), (shape((2 * rows, columns), BF16),))
    count = width // 2 // Z
    parts = call(
        value_grad_body,
        "per_value",
        (here,),
        (*tokens_half, d_value, swap(d_value, "core", CORE)),
        (block(2, count), block(2, count), block(1, count // 2), block(1, count // 2)) + (block(1, count),) * 3,
        vmem=LARGE,
    )
    arrived = start_scatter(*parts[:4])
    terms = end_scatter(arrived, relay(arrived, *parts[4:6]), parts[6])
    small = shape((Z * CORE, 8, 128), F32)
    shard, square = call(
        shard_body,
        "shards",
        (),
        (out_shard, *terms),
        (shape((count, 2 * columns), BF16), small),
        vmem=LARGE,
    )

    halves = shard.reshape(2, count // 2, 2 * columns)
    pairs = ([(0, 0), (1, 2), (2, 1), (3, 3)], [(0, 1), (1, 3), (2, 0), (3, 2)])
    along = [
        [((s // 2 * Z + k) * 2 + s % 2, (t // 2 * Z + k) * 2 + t % 2) for k in range(Z) for s, t in pair]
        for pair in pairs
    ]
    axes = ("yh", "z", "core")
    near = lax.ppermute(pick(halves, image), axes, along[0])
    far = lax.ppermute(pick(halves, 1 - image), axes, along[1])

    squares = lax.all_to_all(square, ("z", "core"), 0, 0, tiled=True)
    (squares,) = call(square_body, "squares", (), (squares,), (small,))
    squares = lax.all_to_all(squares, ("yh", "yl", "x"), 0, 0, tiled=True)
    rows_of_both = shape(noise_value.shape, F32)
    grad_value, grad_out = call(
        final_body,
        "final",
        (this_core,),
        (squares, near, far, noise_value, noise_out.T),
        (rows_of_both, rows_of_both),
    )
    return grad_value, grad_out.T


def solution(mesh):
    fine = Mesh(mesh.devices.reshape(YH, Z, CORE, 2, 4), ("yh", "z", "core", "yl", "x"))
    seq, tensor = ("yh", "z", "core"), ("yl", "x")
    placed = (
        P(None, seq, None),
        P(None, tensor),
        P(None, tensor),
        P(None, tensor),
        P(tensor, None),
        P(None, seq, None),
        P(seq, tensor),
        P(tensor, seq),
    )
    return jax.shard_map(
        local,
        mesh=fine,
        in_specs=placed,
        out_specs=(P(seq, tensor), P(tensor, seq)),
        check_vma=False,
    )
```

```python
import functools
import math

import jax
import jax.numpy as jnp
from jax import lax
from jax.experimental import pallas as pl
from jax.experimental.pallas import tpu as pltpu
from jax.sharding import Mesh, PartitionSpec as P

D = 3072
HEADS = 24
HEAD_DIM = 128
F32 = jnp.float32
BF16 = jnp.bfloat16
YH, Z, CORE = 2, 8, 2
SMALL, LARGE = 24 * 2**20, 60 * 2**20
SCALE = 1.0 / math.sqrt(HEAD_DIM)


def shift(x, axis, size, by):
    return lax.ppermute(x, axis, [(i, (i + by) % size) for i in range(size)])


def shift_by_core(x, by):
    pairs = []
    for place in range(Z):
        pairs.append((place * CORE, (place + by) % Z * CORE))
        pairs.append((place * CORE + 1, (place - by) % Z * CORE + 1))
    return lax.ppermute(x, ("z", "core"), pairs)


def swap(x, axis, size, mask=1):
    return lax.ppermute(x, axis, [(i, i ^ mask) for i in range(size)])


def head_cols(head):
    return slice(head * HEAD_DIM, (head + 1) * HEAD_DIM)


def log_add(left, right):
    top = jnp.maximum(left, right)
    return top + jnp.log(jnp.exp(left - top) + jnp.exp(right - top))


class Arriving:
    def __init__(self, source, target, sem):
        self.copy = pltpu.make_async_copy(source, target, sem)
        self.target, self.here = target, False
        self.copy.start()

    def ref(self):
        if not self.here:
            self.copy.wait()
            self.here = True
        return self.target

    def __getitem__(self, at):
        return self.ref()[at]


class Leaving:
    def __init__(self, source, target, sem):
        self.copy = pltpu.make_async_copy(source, target, sem)
        self.ref, self.sent = source, False

    def send(self):
        if not self.sent:
            self.copy.start()
            self.sent = True


def call(body, name, scalars, inputs, outputs, views=None, vmem=SMALL):
    views = views or {}
    n_scalars, n_inputs, n_outputs = len(scalars), len(inputs), len(outputs)
    shapes = [views[at][0] if at in views else x.shape for at, x in enumerate(inputs)]

    def kernel(*refs):
        numbers, refs = refs[:n_scalars], refs[n_scalars:]
        sources, refs = refs[:n_inputs], refs[n_inputs:]
        targets, refs = refs[:n_outputs], refs[n_outputs:]
        in_sems, out_sems = refs[-2:]
        numbers = [ref[0] for ref in numbers]
        arriving = []
        for at, source in enumerate(sources):
            if at in views:
                source = source.at[views[at][1](*numbers)]
            arriving.append(source if small[at] else Arriving(source, refs[at], in_sems.at[at]))
        leaving = [
            Leaving(refs[n_inputs + at], target, out_sems.at[at])
            for at, target in enumerate(targets)
        ]
        body(numbers, arriving, leaving)
        for at, one in enumerate(arriving):
            if not small[at]:
                one.ref()
        for one in leaving:
            one.send()
        for one in leaving:
            one.copy.wait()

    hbm = pl.BlockSpec(memory_space=pltpu.HBM)
    smem = pl.BlockSpec(memory_space=pltpu.SMEM)
    in_vmem = pl.BlockSpec(memory_space=pltpu.VMEM)
    small = [x.dtype == F32 and x.size <= 2**15 for x in inputs]
    return pl.pallas_call(
        kernel,
        out_shape=tuple(outputs),
        in_specs=[smem] * n_scalars + [in_vmem if one else hbm for one in small],
        out_specs=(hbm,) * n_outputs,
        scratch_shapes=[pltpu.VMEM(size, x.dtype) for size, x in zip(shapes, inputs)]
        + [pltpu.VMEM(x.shape, x.dtype) for x in outputs]
        + [pltpu.SemaphoreType.DMA((n_inputs,)), pltpu.SemaphoreType.DMA((n_outputs,))],
        compiler_params=pltpu.CompilerParams(vmem_limit_bytes=vmem),
        cost_estimate=pl.CostEstimate(flops=1000, bytes_accessed=0, transcendentals=0),
        name=name,
    )(*scalars, *inputs)


def score_block(key_block, query_block):
    last = (((1,), (1,)), ((), ()))
    return lax.dot_general(key_block, query_block, last, preferred_element_type=F32) * SCALE


def stats_body(heads, pieces, numbers, arriving, leaving):
    query, keys, carried = arriving[0], arriving[1 : 1 + pieces], arriving[1 + pieces :]
    rows = []
    for head in range(heads):
        cols = head_cols(head)
        blocks = [score_block(key[:, cols], query[:, cols]) for key in keys]
        tops = [jnp.max(scores, axis=0, keepdims=True) for scores in blocks]
        top = functools.reduce(jnp.maximum, tops)
        total = sum(jnp.sum(jnp.exp(scores - top), axis=0, keepdims=True) for scores in blocks)
        rows.append(top + jnp.log(total))
    rows.append(jnp.zeros((8 - heads, rows[0].shape[1]), F32))
    found = jnp.concatenate(rows, axis=0)
    for one in carried:
        found = log_add(found, one[...])
    leaving[0].ref[...] = found


def both_totals(mine, other):
    other = other[...]
    half = other.shape[1] // 2
    other = jnp.concatenate([other[:, half:], other[:, :half]], axis=1)
    return log_add(mine[...], other)


def d_value_body(heads, distances, numbers, arriving, leaving):
    (here,) = numbers
    query, d_attn, mine, other = arriving[:4]
    keys, pieces = arriving[4:], len(distances)
    out, att = leaving
    half = att.ref.shape[2]
    totals = both_totals(mine, other)

    def scores(head, piece):
        cols = head_cols(head)
        return score_block(keys[piece][:, cols], query[:, cols])

    order = [(head, piece) for head in range(heads) for piece in range(pieces)]
    ahead = scores(*order[0])
    for at, (head, piece) in enumerate(order):
        block = ahead
        if at + 1 < len(order):
            ahead = scores(*order[at + 1])
        cols = head_cols(head)
        probs = jnp.exp(block - totals[head : head + 1, :]).astype(BF16)
        d_value = jnp.dot(probs, d_attn[:, cols], preferred_element_type=F32)
        owner = lax.rem(here + (Z - distances[piece]), Z)
        out.ref[owner, :, cols] = d_value.astype(BF16)
        first = (((0,), (0,)), ((), ()))
        value = keys[piece][:, head_cols(heads + head)]
        term = lax.dot_general(value, probs, first, preferred_element_type=F32)
        attended = term if piece == 0 else attended + term
        if piece == pieces - 1:
            att.ref[0, cols, :] = attended[:, :half].astype(BF16)
            att.ref[1, cols, :] = attended[:, half:].astype(BF16)


def turn_body(numbers, arriving, leaving):
    core, _ = numbers
    keep, send = leaving
    for at, one in enumerate(arriving):
        array = one[...]
        rows, width = array.shape
        low, high = array[:, : width // 2].T, array[:, width // 2 :].T
        to = slice(at * rows, (at + 1) * rows)
        keep.ref[:, to] = jnp.where(core == 0, low, high)
        send.ref[:, to] = jnp.where(core == 0, high, low)


def value_grad_body(numbers, arriving, leaving):
    (here,) = numbers
    mine, other, dv_mine, dv_other = [one.ref() for one in arriving]
    rows = leaving[0].ref.shape[1]
    for output, part, ahead in (
        (2, 0, 4),
        (0, 0, 1),
        (0, 1, 3),
        (1, 0, 7),
        (1, 1, 5),
        (3, 0, 2),
        (4, 0, 6),
        (5, 0, 0),
    ):
        at = pl.ds(pl.multiple_of(lax.rem(here + ahead, Z) * rows, rows), rows)
        product = jnp.dot(mine[at, :], dv_mine[...], preferred_element_type=F32)
        product += jnp.dot(other[at, :], dv_other[...], preferred_element_type=F32)
        leaving[output].ref[part] = product.astype(BF16)
        if part == leaving[output].ref.shape[0] - 1:
            leaving[output].send()


def out_grad_body(numbers, arriving, leaving):
    mine, other, att, att_other = arriving
    (out,) = leaving
    att_mine = (att[0].astype(F32) + att_other[1].astype(F32)).astype(BF16)
    att_rest = (att[1].astype(F32) + att_other[0].astype(F32)).astype(BF16)
    last = (((1,), (1,)), ((), ()))
    rows = out.ref.shape[0] // Z
    for part in range(Z):
        at = slice(part * rows, (part + 1) * rows)
        product = lax.dot_general(mine[at, :], att_mine, last, preferred_element_type=F32)
        product += lax.dot_general(other[at, :], att_rest, last, preferred_element_type=F32)
        out.ref[at, :] = product.astype(BF16)


def relay_body(numbers, arriving, leaving):
    (core,) = numbers
    near_f, near_b, far, keep_f, keep_b = arriving
    for near, keep, send, takes in (
        (near_f, keep_f, leaving[0], core == 0),
        (near_b, keep_b, leaving[1], core == 1),
    ):
        through = near[1].astype(F32) + jnp.where(takes, far[0].astype(F32), 0.0)
        send.ref[0] = (keep[0].astype(F32) + through).astype(BF16)
        send.send()


def total_of(own, near_f, near_b, last_f, last_b):
    near = near_f[0].astype(F32) + near_b[0].astype(F32)
    return own[0].astype(F32) + near + (last_f[0].astype(F32) + last_b[0].astype(F32))


def sum_body(numbers, arriving, leaving):
    total = sum(arriving[0][part].astype(F32) for part in range(Z))
    leaving[0].ref[...] = total.astype(BF16)


def shard_body(numbers, arriving, leaving):
    out, *terms = arriving
    shard, square_out = leaving
    columns = shard.ref.shape[1] // 2
    square = jnp.zeros((1, 1), F32)
    for total, at in ((out[...].astype(F32), columns), (total_of(*terms), 0)):
        shard.ref[:, at : at + columns] = total.astype(BF16)
        column_sums = jnp.sum(total * total, axis=0, keepdims=True)
        square += jnp.sum(column_sums, axis=1, keepdims=True)
    square_out.ref[...] = jnp.broadcast_to(square.reshape(1, 1, 1), square_out.ref.shape)


def sum_parts(parts, first, count):
    return functools.reduce(jnp.add, [parts[first + at] for at in range(count)])


def square_body(numbers, arriving, leaving):
    total = sum_parts(arriving[0], 0, Z * CORE)
    leaving[0].ref[...] = jnp.broadcast_to(total[None], leaving[0].ref.shape)


def final_body(numbers, arriving, leaving):
    (core,) = numbers
    squares, near, far, noise_value, noise_out = arriving
    value, out = leaving
    columns = value.ref.shape[1]
    clip_bound = math.sqrt(2.0 * D * HEADS * HEAD_DIM)
    factors = []
    for image in range(YH):
        total = sum_parts(squares, image * 8, 8)[0:1, 0:1]
        factors.append(clip_bound / (jnp.sqrt(total) + 0.01))
    near_factor = jnp.where(core == 0, factors[0], factors[1])
    far_factor = jnp.where(core == 0, factors[1], factors[0])
    weighted = near_factor * near[...].astype(F32) + far_factor * far[...].astype(F32)
    value.ref[...] = (weighted[:, :columns] + noise_value[...]) * 0.5
    out.ref[...] = (weighted[:, columns:] + noise_out[...]) * 0.5


def local(tokens, w_query, w_key, w_value, w_out, cotangent, noise_value, noise_out):
    images, rows, width = tokens.shape
    columns = w_query.shape[1]
    heads = columns // HEAD_DIM
    image = lax.axis_index("yh")
    z = lax.axis_index("z")
    core = lax.axis_index("core")
    flat_tokens = tokens.reshape(images * rows, width)
    flat_cotangent = cotangent.reshape(images * rows, width)
    shape = jax.ShapeDtypeStruct
    here, this_core, this_image = z.reshape(1), core.reshape(1), image.reshape(1)

    def project(weight):
        return jnp.dot(flat_tokens, weight, preferred_element_type=F32).astype(BF16)

    def pick(array, index):
        return lax.dynamic_index_in_dim(array, index, 0, keepdims=False)

    def image_rows(array):
        array = array.reshape(images, rows, array.shape[1])
        partner = swap(pick(array, 1 - image), "yh", YH)
        return jnp.concatenate([pick(array, image), partner], axis=0)

    def from_partner(array):
        return lax.all_gather(pick(array, 1 - image), "yh", axis=0)

    keys_values = jnp.concatenate([project(w_key), project(w_value)], axis=1)
    chunk = image_rows(keys_values)
    d_attn = jnp.einsum("rd,cd->rc", flat_cotangent, w_out, preferred_element_type=F32)
    queries_d = jnp.concatenate([project(w_query), d_attn.astype(BF16)], axis=1)
    chunk, queries_d = lax.optimization_barrier((chunk, queries_d))
    queries_d = image_rows(queries_d)
    chip_rows = CORE * images * rows

    def stats_of(chosen, *carried):
        (found,) = call(
            functools.partial(stats_body, heads, len(chosen)),
            "stats",
            (),
            (queries_d, *chosen, *carried),
            (shape((8, chip_rows), F32),),
            {at: left_part(x) for at, x in enumerate((queries_d, *chosen))},
        )
        return found

    def left_part(x):
        return (x.shape[0], columns), lambda *_: (slice(None), slice(0, columns))

    def right_part(x):
        return (x.shape[0], columns), lambda *_: (slice(None), slice(columns, 2 * columns))

    forward = backward = chunk
    pieces = [chunk]
    for step in range(1, 4):
        forward = shift(forward, "z", Z, 1)
        backward = shift(backward, "z", Z, -1)
        pieces += [forward, backward]
        if step == 1:
            forward, backward, queries_d, late_tokens, late_cotangent = lax.optimization_barrier(
                (forward, backward, queries_d, tokens, cotangent)
            )
            queries_d = jnp.concatenate([queries_d, swap(queries_d, "core", CORE)], axis=0)
            cotangent_pair = cotangent, from_partner(late_cotangent)
            tokens_pair = tokens, from_partner(late_tokens)
        if step == 3:
            stats = stats_of(pieces[:3])
            forward, backward, stats = lax.optimization_barrier((forward, backward, stats))
    pieces.append(shift_by_core(jnp.where(core == 0, forward, backward), 1))
    stats = stats_of(pieces[3:7], stats)
    stats = stats_of(pieces[7:], stats)
    other_stats = swap(stats, "core", CORE)

    def block(parts, count):
        return shape((parts, count, columns), BF16)

    def start_scatter(near_f, near_b, far):
        return shift(near_f, "z", Z, 1), shift(near_b, "z", Z, -1), shift_by_core(far, 2)

    def relay(arrived, keep_f, keep_b):
        like = shape(keep_f.shape, BF16)
        return call(
            relay_body,
            "relay",
            (this_core,),
            (*arrived, keep_f, keep_b),
            (like, like),
            vmem=LARGE,
        )

    def end_scatter(arrived, sums, own):
        return own, arrived[0], arrived[1], shift(sums[0], "z", Z, 2), shift(sums[1], "z", Z, -2)

    distances = (0, 1, 7, 2, 6, 3, 5, 4)
    d_value, attended = call(
        functools.partial(d_value_body, heads, distances),
        "d_value",
        (here,),
        (queries_d, queries_d, stats, other_stats, *pieces),
        (block(Z, 2 * rows), shape((2, columns, chip_rows // 2), BF16)),
        {0: left_part(queries_d), 1: right_part(queries_d)},
        LARGE,
    )
    attended, cotangent_pair = lax.optimization_barrier((attended, cotangent_pair))
    terms = lax.all_to_all(d_value, "z", 0, 0, tiled=True)
    attended_other = swap(attended, "core", CORE)

    def half_width(pair):
        turned = shape((width // 2, 2 * rows), BF16)
        keep, send = call(
            turn_body,
            "turn",
            (this_core, this_image),
            pair,
            (turned, turned),
            {
                0: ((rows, width), lambda core, image: image),
                1: ((rows, width), lambda core, image: 1 - image),
            },
            LARGE,
        )
        return keep, swap(send, "core", CORE)

    cotangent_half = half_width(cotangent_pair)
    (per_out,) = call(
        out_grad_body,
        "per_out",
        (),
        (*cotangent_half, attended, attended_other),
        (shape((width // 2, columns), BF16),),
        vmem=LARGE,
    )
    per_out, tokens_pair = lax.optimization_barrier((per_out, tokens_pair))
    out_shard = lax.psum_scatter(per_out, "z", scatter_dimension=0, tiled=True)
    tokens_half = half_width(tokens_pair)

    (d_value,) = call(sum_body, "d_value_sum", (), (terms,), (shape((2 * rows, columns), BF16),))
    count = width // 2 // Z
    parts = call(
        value_grad_body,
        "per_value",
        (here,),
        (*tokens_half, d_value, swap(d_value, "core", CORE)),
        (block(2, count), block(2, count)) + (block(1, count),) * 4,
        vmem=LARGE,
    )
    arrived = start_scatter(*parts[:3])
    terms = end_scatter(arrived, relay(arrived, *parts[3:5]), parts[5])
    small = shape((Z * CORE, 8, 128), F32)
    shard, square = call(
        shard_body,
        "shards",
        (),
        (out_shard, *terms),
        (shape((count, 2 * columns), BF16), small),
        vmem=LARGE,
    )

    halves = shard.reshape(2, count // 2, 2 * columns)
    pairs = ([(0, 0), (1, 2), (2, 1), (3, 3)], [(0, 1), (1, 3), (2, 0), (3, 2)])
    along = [
        [((s // 2 * Z + k) * 2 + s % 2, (t // 2 * Z + k) * 2 + t % 2) for k in range(Z) for s, t in pair]
        for pair in pairs
    ]
    axes = ("yh", "z", "core")
    near = lax.ppermute(pick(halves, image), axes, along[0])
    far = lax.ppermute(pick(halves, 1 - image), axes, along[1])

    squares = lax.all_to_all(square, ("z", "core"), 0, 0, tiled=True)
    (squares,) = call(square_body, "squares", (), (squares,), (small,))
    squares = lax.all_to_all(squares, ("yh", "yl", "x"), 0, 0, tiled=True)
    rows_of_both = shape(noise_value.shape, F32)
    grad_value, grad_out = call(
        final_body,
        "final",
        (this_core,),
        (squares, near, far, noise_value, noise_out.T),
        (rows_of_both, rows_of_both),
    )
    return grad_value, grad_out.T


def solution(mesh):
    fine = Mesh(mesh.devices.reshape(YH, Z, CORE, 2, 4), ("yh", "z", "core", "yl", "x"))
    seq, tensor = ("yh", "z", "core"), ("yl", "x")
    placed = (
        P(None, seq, None),
        P(None, tensor),
        P(None, tensor),
        P(None, tensor),
        P(tensor, None),
        P(None, seq, None),
        P(seq, tensor),
        P(tensor, seq),
    )
    return jax.shard_map(
        local,
        mesh=fine,
        in_specs=placed,
        out_specs=(P(seq, tensor), P(tensor, seq)),
        check_vma=False,
    )
```

```python
import functools
import math

import jax
import jax.numpy as jnp
from jax import lax
from jax.experimental import pallas as pl
from jax.experimental.pallas import tpu as pltpu
from jax.sharding import Mesh, PartitionSpec as P

D = 3072
HEADS = 24
HEAD_DIM = 128
F32 = jnp.float32
BF16 = jnp.bfloat16
YH, Z, CORE = 2, 8, 2
SMALL, LARGE = 24 * 2**20, 60 * 2**20
SCALE = 1.0 / math.sqrt(HEAD_DIM)


def shift(x, axis, size, by):
    return lax.ppermute(x, axis, [(i, (i + by) % size) for i in range(size)])


def shift_by_core(x, by):
    pairs = []
    for place in range(Z):
        pairs.append((place * CORE, (place + by) % Z * CORE))
        pairs.append((place * CORE + 1, (place - by) % Z * CORE + 1))
    return lax.ppermute(x, ("z", "core"), pairs)


def swap(x, axis, size, mask=1):
    return lax.ppermute(x, axis, [(i, i ^ mask) for i in range(size)])


def head_cols(head):
    return slice(head * HEAD_DIM, (head + 1) * HEAD_DIM)


def log_add(left, right):
    top = jnp.maximum(left, right)
    return top + jnp.log(jnp.exp(left - top) + jnp.exp(right - top))


class Arriving:
    def __init__(self, source, target, sem):
        self.copy = pltpu.make_async_copy(source, target, sem)
        self.target, self.here = target, False
        self.copy.start()

    def ref(self):
        if not self.here:
            self.copy.wait()
            self.here = True
        return self.target

    def __getitem__(self, at):
        return self.ref()[at]


class Leaving:
    def __init__(self, source, target, sem):
        self.copy = pltpu.make_async_copy(source, target, sem)
        self.ref, self.sent = source, False

    def send(self):
        if not self.sent:
            self.copy.start()
            self.sent = True


def call(body, name, scalars, inputs, outputs, views=None, vmem=SMALL):
    views = views or {}
    n_scalars, n_inputs, n_outputs = len(scalars), len(inputs), len(outputs)
    shapes = [views[at][0] if at in views else x.shape for at, x in enumerate(inputs)]

    def kernel(*refs):
        numbers, refs = refs[:n_scalars], refs[n_scalars:]
        sources, refs = refs[:n_inputs], refs[n_inputs:]
        targets, refs = refs[:n_outputs], refs[n_outputs:]
        in_sems, out_sems = refs[-2:]
        numbers = [ref[0] for ref in numbers]
        arriving = []
        for at, source in enumerate(sources):
            if at in views:
                source = source.at[views[at][1](*numbers)]
            arriving.append(source if small[at] else Arriving(source, refs[at], in_sems.at[at]))
        leaving = [
            Leaving(refs[n_inputs + at], target, out_sems.at[at])
            for at, target in enumerate(targets)
        ]
        body(numbers, arriving, leaving)
        for at, one in enumerate(arriving):
            if not small[at]:
                one.ref()
        for one in leaving:
            one.send()
        for one in leaving:
            one.copy.wait()

    hbm = pl.BlockSpec(memory_space=pltpu.HBM)
    smem = pl.BlockSpec(memory_space=pltpu.SMEM)
    in_vmem = pl.BlockSpec(memory_space=pltpu.VMEM)
    small = [x.dtype == F32 and x.size <= 2**15 for x in inputs]
    return pl.pallas_call(
        kernel,
        out_shape=tuple(outputs),
        in_specs=[smem] * n_scalars + [in_vmem if one else hbm for one in small],
        out_specs=(hbm,) * n_outputs,
        scratch_shapes=[pltpu.VMEM(size, x.dtype) for size, x in zip(shapes, inputs)]
        + [pltpu.VMEM(x.shape, x.dtype) for x in outputs]
        + [pltpu.SemaphoreType.DMA((n_inputs,)), pltpu.SemaphoreType.DMA((n_outputs,))],
        compiler_params=pltpu.CompilerParams(vmem_limit_bytes=vmem),
        cost_estimate=pl.CostEstimate(flops=1000, bytes_accessed=0, transcendentals=0),
        name=name,
    )(*scalars, *inputs)


def score_block(key_block, query_block):
    last = (((1,), (1,)), ((), ()))
    return lax.dot_general(key_block, query_block, last, preferred_element_type=F32) * SCALE


def stats_body(heads, pieces, numbers, arriving, leaving):
    query, keys, carried = arriving[0], arriving[1 : 1 + pieces], arriving[1 + pieces :]
    rows = []
    for head in range(heads):
        cols = head_cols(head)
        blocks = [score_block(key[:, cols], query[:, cols]) for key in keys]
        tops = [jnp.max(scores, axis=0, keepdims=True) for scores in blocks]
        top = functools.reduce(jnp.maximum, tops)
        total = sum(jnp.sum(jnp.exp(scores - top), axis=0, keepdims=True) for scores in blocks)
        rows.append(top + jnp.log(total))
    rows.append(jnp.zeros((8 - heads, rows[0].shape[1]), F32))
    found = jnp.concatenate(rows, axis=0)
    for one in carried:
        found = log_add(found, one[...])
    leaving[0].ref[...] = found


def both_totals(mine, other):
    other = other[...]
    half = other.shape[1] // 2
    other = jnp.concatenate([other[:, half:], other[:, :half]], axis=1)
    return log_add(mine[...], other)


def d_value_body(heads, distances, numbers, arriving, leaving):
    (here,) = numbers
    query, d_attn, mine, other = arriving[:4]
    keys, pieces = arriving[4:], len(distances)
    out, att = leaving
    half = att.ref.shape[2]
    totals = both_totals(mine, other)

    def scores(head, piece):
        cols = head_cols(head)
        return score_block(keys[piece][:, cols], query[:, cols])

    order = [(head, piece) for head in range(heads) for piece in range(pieces)]
    ahead = scores(*order[0])
    for at, (head, piece) in enumerate(order):
        block = ahead
        if at + 1 < len(order):
            ahead = scores(*order[at + 1])
        cols = head_cols(head)
        probs = jnp.exp(block - totals[head : head + 1, :]).astype(BF16)
        d_value = jnp.dot(probs, d_attn[:, cols], preferred_element_type=F32)
        owner = lax.rem(here + (Z - distances[piece]), Z)
        out.ref[owner, :, cols] = d_value.astype(BF16)
        first = (((0,), (0,)), ((), ()))
        value = keys[piece][:, head_cols(heads + head)]
        term = lax.dot_general(value, probs, first, preferred_element_type=F32)
        attended = term if piece == 0 else attended + term
        if piece == pieces - 1:
            att.ref[0, cols, :] = attended[:, :half].astype(BF16)
            att.ref[1, cols, :] = attended[:, half:].astype(BF16)


def turn_body(numbers, arriving, leaving):
    core, _ = numbers
    keep, send = leaving
    for at, one in enumerate(arriving):
        array = one[...]
        rows, width = array.shape
        low, high = array[:, : width // 2].T, array[:, width // 2 :].T
        to = slice(at * rows, (at + 1) * rows)
        keep.ref[:, to] = jnp.where(core == 0, low, high)
        send.ref[:, to] = jnp.where(core == 0, high, low)


def value_grad_body(numbers, arriving, leaving):
    (here,) = numbers
    mine, other, dv_mine, dv_other = [one.ref() for one in arriving]
    rows = leaving[0].ref.shape[1]
    for output, part, ahead in (
        (2, 0, 4),
        (0, 0, 1),
        (0, 1, 3),
        (1, 0, 7),
        (1, 1, 5),
        (3, 0, 2),
        (4, 0, 6),
        (5, 0, 0),
    ):
        at = pl.ds(pl.multiple_of(lax.rem(here + ahead, Z) * rows, rows), rows)
        product = jnp.dot(mine[at, :], dv_mine[...], preferred_element_type=F32)
        product += jnp.dot(other[at, :], dv_other[...], preferred_element_type=F32)
        leaving[output].ref[part] = product.astype(BF16)
        if part == leaving[output].ref.shape[0] - 1:
            leaving[output].send()


def out_grad_body(numbers, arriving, leaving):
    mine, other, att, att_other = arriving
    (out,) = leaving
    att_mine = (att[0].astype(F32) + att_other[1].astype(F32)).astype(BF16)
    att_rest = (att[1].astype(F32) + att_other[0].astype(F32)).astype(BF16)
    last = (((1,), (1,)), ((), ()))
    rows = out.ref.shape[0] // Z
    for part in range(Z):
        at = slice(part * rows, (part + 1) * rows)
        product = lax.dot_general(mine[at, :], att_mine, last, preferred_element_type=F32)
        product += lax.dot_general(other[at, :], att_rest, last, preferred_element_type=F32)
        out.ref[at, :] = product.astype(BF16)


def relay_body(numbers, arriving, leaving):
    (core,) = numbers
    near_f, near_b, far, keep_f, keep_b = arriving
    for near, keep, send, takes in (
        (near_f, keep_f, leaving[0], core == 0),
        (near_b, keep_b, leaving[1], core == 1),
    ):
        through = near[1].astype(F32) + jnp.where(takes, far[0].astype(F32), 0.0)
        send.ref[0] = (keep[0].astype(F32) + through).astype(BF16)
        send.send()


def total_of(own, near_f, near_b, last_f, last_b):
    near = near_f[0].astype(F32) + near_b[0].astype(F32)
    return own[0].astype(F32) + near + (last_f[0].astype(F32) + last_b[0].astype(F32))


def sum_body(numbers, arriving, leaving):
    total = sum(arriving[0][part].astype(F32) for part in range(Z))
    leaving[0].ref[...] = total.astype(BF16)


def shard_body(numbers, arriving, leaving):
    (image,) = numbers
    out, *terms = arriving
    first, second, square_out = leaving
    rows, columns = first.ref.shape[0], first.ref.shape[1] // 2
    square = jnp.zeros((1, 1), F32)
    for total, at in ((out[...].astype(F32), columns), (total_of(*terms), 0)):
        top, bottom = total[:rows].astype(BF16), total[rows:].astype(BF16)
        first.ref[:, at : at + columns] = jnp.where(image == 0, top, bottom)
        second.ref[:, at : at + columns] = jnp.where(image == 0, bottom, top)
        column_sums = jnp.sum(total * total, axis=0, keepdims=True)
        square += jnp.sum(column_sums, axis=1, keepdims=True)
    first.send()
    second.send()
    square_out.ref[...] = jnp.broadcast_to(square.reshape(1, 1, 1), square_out.ref.shape)


def sum_parts(parts, first, count):
    return functools.reduce(jnp.add, [parts[first + at] for at in range(count)])


def square_body(numbers, arriving, leaving):
    total = sum_parts(arriving[0], 0, Z * CORE)
    leaving[0].ref[...] = jnp.broadcast_to(total[None], leaving[0].ref.shape)


def final_body(numbers, arriving, leaving):
    (core,) = numbers
    squares, near, far, noise_value, noise_out = arriving
    value, out = leaving
    columns = value.ref.shape[1]
    clip_bound = math.sqrt(2.0 * D * HEADS * HEAD_DIM)
    factors = []
    for image in range(YH):
        total = sum_parts(squares, image * 8, 8)[0:1, 0:1]
        factors.append(clip_bound / (jnp.sqrt(total) + 0.01))
    near_factor = jnp.where(core == 0, factors[0], factors[1])
    far_factor = jnp.where(core == 0, factors[1], factors[0])
    weighted = near_factor * near[...].astype(F32) + far_factor * far[...].astype(F32)
    value.ref[...] = (weighted[:, :columns] + noise_value[...]) * 0.5
    out.ref[...] = (weighted[:, columns:] + noise_out[...]) * 0.5


def local(tokens, w_query, w_key, w_value, w_out, cotangent, noise_value, noise_out):
    images, rows, width = tokens.shape
    columns = w_query.shape[1]
    heads = columns // HEAD_DIM
    image = lax.axis_index("yh")
    z = lax.axis_index("z")
    core = lax.axis_index("core")
    flat_tokens = tokens.reshape(images * rows, width)
    flat_cotangent = cotangent.reshape(images * rows, width)
    shape = jax.ShapeDtypeStruct
    here, this_core, this_image = z.reshape(1), core.reshape(1), image.reshape(1)

    def project(weight):
        return jnp.dot(flat_tokens, weight, preferred_element_type=F32).astype(BF16)

    def pick(array, index):
        return lax.dynamic_index_in_dim(array, index, 0, keepdims=False)

    def image_rows(array):
        array = array.reshape(images, rows, array.shape[1])
        partner = swap(pick(array, 1 - image), "yh", YH)
        return jnp.concatenate([pick(array, image), partner], axis=0)

    def from_partner(array):
        return lax.all_gather(pick(array, 1 - image), "yh", axis=0)

    keys_values = jnp.concatenate([project(w_key), project(w_value)], axis=1)
    chunk = image_rows(keys_values)
    d_attn = jnp.einsum("rd,cd->rc", flat_cotangent, w_out, preferred_element_type=F32)
    queries_d = jnp.concatenate([project(w_query), d_attn.astype(BF16)], axis=1)
    chunk, queries_d = lax.optimization_barrier((chunk, queries_d))
    queries_d = image_rows(queries_d)
    chip_rows = CORE * images * rows

    def stats_of(chosen, *carried):
        (found,) = call(
            functools.partial(stats_body, heads, len(chosen)),
            "stats",
            (),
            (queries_d, *chosen, *carried),
            (shape((8, chip_rows), F32),),
            {at: left_part(x) for at, x in enumerate((queries_d, *chosen))},
        )
        return found

    def left_part(x):
        return (x.shape[0], columns), lambda *_: (slice(None), slice(0, columns))

    def right_part(x):
        return (x.shape[0], columns), lambda *_: (slice(None), slice(columns, 2 * columns))

    forward = backward = chunk
    pieces = [chunk]
    for step in range(1, 4):
        forward = shift(forward, "z", Z, 1)
        backward = shift(backward, "z", Z, -1)
        pieces += [forward, backward]
        if step == 1:
            forward, backward, queries_d, late_tokens, late_cotangent = lax.optimization_barrier(
                (forward, backward, queries_d, tokens, cotangent)
            )
            queries_d = jnp.concatenate([queries_d, swap(queries_d, "core", CORE)], axis=0)
            cotangent_pair = cotangent, from_partner(late_cotangent)
            tokens_pair = tokens, from_partner(late_tokens)
        if step == 3:
            stats = stats_of(pieces[:3])
            forward, backward, stats = lax.optimization_barrier((forward, backward, stats))
    pieces.append(shift_by_core(jnp.where(core == 0, forward, backward), 1))
    stats = stats_of(pieces[3:7], stats)
    stats = stats_of(pieces[7:], stats)
    other_stats = swap(stats, "core", CORE)

    def block(parts, count):
        return shape((parts, count, columns), BF16)

    def start_scatter(near_f, near_b, far):
        return shift(near_f, "z", Z, 1), shift(near_b, "z", Z, -1), shift_by_core(far, 2)

    def relay(arrived, keep_f, keep_b):
        like = shape(keep_f.shape, BF16)
        return call(
            relay_body,
            "relay",
            (this_core,),
            (*arrived, keep_f, keep_b),
            (like, like),
            vmem=LARGE,
        )

    def end_scatter(arrived, sums, own):
        return own, arrived[0], arrived[1], shift(sums[0], "z", Z, 2), shift(sums[1], "z", Z, -2)

    distances = (0, 1, 7, 2, 6, 3, 5, 4)
    d_value, attended = call(
        functools.partial(d_value_body, heads, distances),
        "d_value",
        (here,),
        (queries_d, queries_d, stats, other_stats, *pieces),
        (block(Z, 2 * rows), shape((2, columns, chip_rows // 2), BF16)),
        {0: left_part(queries_d), 1: right_part(queries_d)},
        LARGE,
    )
    attended, cotangent_pair = lax.optimization_barrier((attended, cotangent_pair))
    terms = lax.all_to_all(d_value, "z", 0, 0, tiled=True)
    attended_other = swap(attended, "core", CORE)

    def half_width(pair):
        turned = shape((width // 2, 2 * rows), BF16)
        keep, send = call(
            turn_body,
            "turn",
            (this_core, this_image),
            pair,
            (turned, turned),
            {
                0: ((rows, width), lambda core, image: image),
                1: ((rows, width), lambda core, image: 1 - image),
            },
            LARGE,
        )
        return keep, swap(send, "core", CORE)

    cotangent_half = half_width(cotangent_pair)
    (per_out,) = call(
        out_grad_body,
        "per_out",
        (),
        (*cotangent_half, attended, attended_other),
        (shape((width // 2, columns), BF16),),
        vmem=LARGE,
    )
    per_out, tokens_pair = lax.optimization_barrier((per_out, tokens_pair))
    out_shard = lax.psum_scatter(per_out, "z", scatter_dimension=0, tiled=True)
    tokens_half = half_width(tokens_pair)

    (d_value,) = call(sum_body, "d_value_sum", (), (terms,), (shape((2 * rows, columns), BF16),))
    count = width // 2 // Z
    parts = call(
        value_grad_body,
        "per_value",
        (here,),
        (*tokens_half, d_value, swap(d_value, "core", CORE)),
        (block(2, count), block(2, count)) + (block(1, count),) * 4,
        vmem=LARGE,
    )
    arrived = start_scatter(*parts[:3])
    terms = end_scatter(arrived, relay(arrived, *parts[3:5]), parts[5])
    small = shape((Z * CORE, 8, 128), F32)
    half = shape((count // 2, 2 * columns), BF16)
    first, second, square = call(
        shard_body,
        "shards",
        (this_image,),
        (out_shard, *terms),
        (half, half, small),
        vmem=LARGE,
    )

    pairs = ([(0, 0), (1, 2), (2, 1), (3, 3)], [(0, 1), (1, 3), (2, 0), (3, 2)])
    along = [
        [((s // 2 * Z + k) * 2 + s % 2, (t // 2 * Z + k) * 2 + t % 2) for k in range(Z) for s, t in pair]
        for pair in pairs
    ]
    axes = ("yh", "z", "core")
    near = lax.ppermute(first, axes, along[0])
    far = lax.ppermute(second, axes, along[1])

    squares = lax.all_to_all(square, ("z", "core"), 0, 0, tiled=True)
    (squares,) = call(square_body, "squares", (), (squares,), (small,))
    squares = lax.all_to_all(squares, ("yh", "yl", "x"), 0, 0, tiled=True)
    rows_of_both = shape(noise_value.shape, F32)
    grad_value, grad_out = call(
        final_body,
        "final",
        (this_core,),
        (squares, near, far, noise_value, noise_out.T),
        (rows_of_both, rows_of_both),
    )
    return grad_value, grad_out.T


def solution(mesh):
    fine = Mesh(mesh.devices.reshape(YH, Z, CORE, 2, 4), ("yh", "z", "core", "yl", "x"))
    seq, tensor = ("yh", "z", "core"), ("yl", "x")
    placed = (
        P(None, seq, None),
        P(None, tensor),
        P(None, tensor),
        P(None, tensor),
        P(tensor, None),
        P(None, seq, None),
        P(seq, tensor),
        P(tensor, seq),
    )
    return jax.shard_map(
        local,
        mesh=fine,
        in_specs=placed,
        out_specs=(P(seq, tensor), P(tensor, seq)),
        check_vma=False,
    )
```

```python
import functools
import math

import jax
import jax.numpy as jnp
from jax import lax
from jax.experimental import pallas as pl
from jax.experimental.pallas import tpu as pltpu
from jax.sharding import Mesh, PartitionSpec as P

D = 3072
HEADS = 24
HEAD_DIM = 128
F32 = jnp.float32
BF16 = jnp.bfloat16
YH, Z, CORE = 2, 8, 2
SMALL, LARGE = 24 * 2**20, 60 * 2**20
SCALE = 1.0 / math.sqrt(HEAD_DIM)


def shift(x, axis, size, by):
    return lax.ppermute(x, axis, [(i, (i + by) % size) for i in range(size)])


def shift_by_core(x, by):
    pairs = []
    for place in range(Z):
        pairs.append((place * CORE, (place + by) % Z * CORE))
        pairs.append((place * CORE + 1, (place - by) % Z * CORE + 1))
    return lax.ppermute(x, ("z", "core"), pairs)


def swap(x, axis, size, mask=1):
    return lax.ppermute(x, axis, [(i, i ^ mask) for i in range(size)])


def head_cols(head):
    return slice(head * HEAD_DIM, (head + 1) * HEAD_DIM)


def log_add(left, right):
    top = jnp.maximum(left, right)
    return top + jnp.log(jnp.exp(left - top) + jnp.exp(right - top))


class Arriving:
    def __init__(self, source, target, sem):
        self.copy = pltpu.make_async_copy(source, target, sem)
        self.target, self.here = target, False
        self.copy.start()

    def ref(self):
        if not self.here:
            self.copy.wait()
            self.here = True
        return self.target

    def __getitem__(self, at):
        return self.ref()[at]


class Leaving:
    def __init__(self, source, target, sem):
        self.copy = pltpu.make_async_copy(source, target, sem)
        self.ref, self.sent = source, False

    def send(self):
        if not self.sent:
            self.copy.start()
            self.sent = True


def call(body, name, scalars, inputs, outputs, views=None, vmem=SMALL):
    views = views or {}
    n_scalars, n_inputs, n_outputs = len(scalars), len(inputs), len(outputs)
    shapes = [views[at][0] if at in views else x.shape for at, x in enumerate(inputs)]

    def kernel(*refs):
        numbers, refs = refs[:n_scalars], refs[n_scalars:]
        sources, refs = refs[:n_inputs], refs[n_inputs:]
        targets, refs = refs[:n_outputs], refs[n_outputs:]
        in_sems, out_sems = refs[-2:]
        numbers = [ref[0] for ref in numbers]
        arriving = []
        for at, source in enumerate(sources):
            if at in views:
                source = source.at[views[at][1](*numbers)]
            arriving.append(source if small[at] else Arriving(source, refs[at], in_sems.at[at]))
        leaving = [
            Leaving(refs[n_inputs + at], target, out_sems.at[at])
            for at, target in enumerate(targets)
        ]
        body(numbers, arriving, leaving)
        for at, one in enumerate(arriving):
            if not small[at]:
                one.ref()
        for one in leaving:
            one.send()
        for one in leaving:
            one.copy.wait()

    hbm = pl.BlockSpec(memory_space=pltpu.HBM)
    smem = pl.BlockSpec(memory_space=pltpu.SMEM)
    in_vmem = pl.BlockSpec(memory_space=pltpu.VMEM)
    small = [x.dtype == F32 and x.size <= 2**15 for x in inputs]
    return pl.pallas_call(
        kernel,
        out_shape=tuple(outputs),
        in_specs=[smem] * n_scalars + [in_vmem if one else hbm for one in small],
        out_specs=(hbm,) * n_outputs,
        scratch_shapes=[pltpu.VMEM(size, x.dtype) for size, x in zip(shapes, inputs)]
        + [pltpu.VMEM(x.shape, x.dtype) for x in outputs]
        + [pltpu.SemaphoreType.DMA((n_inputs,)), pltpu.SemaphoreType.DMA((n_outputs,))],
        compiler_params=pltpu.CompilerParams(vmem_limit_bytes=vmem),
        cost_estimate=pl.CostEstimate(flops=1000, bytes_accessed=0, transcendentals=0),
        name=name,
    )(*scalars, *inputs)


def score_block(key_block, query_block):
    last = (((1,), (1,)), ((), ()))
    return lax.dot_general(key_block, query_block, last, preferred_element_type=F32) * SCALE


def stats_body(heads, pieces, numbers, arriving, leaving):
    query, keys, carried = arriving[0], arriving[1 : 1 + pieces], arriving[1 + pieces :]
    rows = []
    for head in range(heads):
        cols = head_cols(head)
        blocks = [score_block(key[:, cols], query[:, cols]) for key in keys]
        tops = [jnp.max(scores, axis=0, keepdims=True) for scores in blocks]
        top = functools.reduce(jnp.maximum, tops)
        total = sum(jnp.sum(jnp.exp(scores - top), axis=0, keepdims=True) for scores in blocks)
        rows.append(top + jnp.log(total))
    rows.append(jnp.zeros((8 - heads, rows[0].shape[1]), F32))
    found = jnp.concatenate(rows, axis=0)
    for one in carried:
        found = log_add(found, one[...])
    leaving[0].ref[...] = found


def both_totals(mine, other):
    other = other[...]
    half = other.shape[1] // 2
    other = jnp.concatenate([other[:, half:], other[:, :half]], axis=1)
    return log_add(mine[...], other)


def d_value_body(heads, distances, numbers, arriving, leaving):
    (here,) = numbers
    query, d_attn, mine, other = arriving[:4]
    keys, pieces = arriving[4:], len(distances)
    out, att = leaving
    half = att.ref.shape[2]
    totals = both_totals(mine, other)

    def scores(head, piece):
        cols = head_cols(head)
        return score_block(keys[piece][:, cols], query[:, cols])

    order = [(head, piece) for head in range(heads) for piece in range(pieces)]
    ahead = scores(*order[0])
    for at, (head, piece) in enumerate(order):
        block = ahead
        if at + 1 < len(order):
            ahead = scores(*order[at + 1])
        cols = head_cols(head)
        probs = jnp.exp(block - totals[head : head + 1, :]).astype(BF16)
        d_value = jnp.dot(probs, d_attn[:, cols], preferred_element_type=F32)
        owner = lax.rem(here + (Z - distances[piece]), Z)
        out.ref[owner, :, cols] = d_value.astype(BF16)
        first = (((0,), (0,)), ((), ()))
        value = keys[piece][:, head_cols(heads + head)]
        term = lax.dot_general(value, probs, first, preferred_element_type=F32)
        attended = term if piece == 0 else attended + term
        if piece == pieces - 1:
            att.ref[0, cols, :] = attended[:, :half].astype(BF16)
            att.ref[1, cols, :] = attended[:, half:].astype(BF16)


def turn_body(numbers, arriving, leaving):
    core, _ = numbers
    keep, send = leaving
    for at, one in enumerate(arriving):
        array = one[...]
        rows, width = array.shape
        low, high = array[:, : width // 2].T, array[:, width // 2 :].T
        to = slice(at * rows, (at + 1) * rows)
        keep.ref[:, to] = jnp.where(core == 0, low, high)
        send.ref[:, to] = jnp.where(core == 0, high, low)


def value_grad_body(numbers, arriving, leaving):
    (here,) = numbers
    mine, other, dv_mine, dv_other = [one.ref() for one in arriving]
    rows = leaving[0].ref.shape[1]
    for output, part, ahead in (
        (2, 0, 4),
        (0, 0, 1),
        (0, 1, 3),
        (1, 0, 7),
        (1, 1, 5),
        (3, 0, 2),
        (4, 0, 6),
        (5, 0, 0),
    ):
        at = pl.ds(pl.multiple_of(lax.rem(here + ahead, Z) * rows, rows), rows)
        product = jnp.dot(mine[at, :], dv_mine[...], preferred_element_type=F32)
        product += jnp.dot(other[at, :], dv_other[...], preferred_element_type=F32)
        leaving[output].ref[part] = product.astype(BF16)
        if part == leaving[output].ref.shape[0] - 1:
            leaving[output].send()


def out_grad_body(numbers, arriving, leaving):
    mine, other, att, att_other = arriving
    (out,) = leaving
    att_mine = (att[0].astype(F32) + att_other[1].astype(F32)).astype(BF16)
    att_rest = (att[1].astype(F32) + att_other[0].astype(F32)).astype(BF16)
    last = (((1,), (1,)), ((), ()))
    rows = out.ref.shape[0] // Z
    for part in range(Z):
        at = slice(part * rows, (part + 1) * rows)
        product = lax.dot_general(mine[at, :], att_mine, last, preferred_element_type=F32)
        product += lax.dot_general(other[at, :], att_rest, last, preferred_element_type=F32)
        out.ref[at, :] = product.astype(BF16)


def relay_body(numbers, arriving, leaving):
    (core,) = numbers
    near_f, near_b, far, keep_f, keep_b = arriving
    for near, keep, send, takes in (
        (near_f, keep_f, leaving[0], core == 0),
        (near_b, keep_b, leaving[1], core == 1),
    ):
        through = near[1].astype(F32) + jnp.where(takes, far[0].astype(F32), 0.0)
        send.ref[0] = (keep[0].astype(F32) + through).astype(BF16)
        send.send()


def total_of(own, near_f, near_b, last_f, last_b):
    near = near_f[0].astype(F32) + near_b[0].astype(F32)
    return own[0].astype(F32) + near + (last_f[0].astype(F32) + last_b[0].astype(F32))


def sum_body(numbers, arriving, leaving):
    total = sum(arriving[0][part].astype(F32) for part in range(Z))
    leaving[0].ref[...] = total.astype(BF16)


def shard_body(numbers, arriving, leaving):
    out, *terms = arriving
    shard, square_out = leaving
    columns = shard.ref.shape[1] // 2
    square = jnp.zeros((1, 1), F32)
    for total, at in ((out[...].astype(F32), columns), (total_of(*terms), 0)):
        shard.ref[:, at : at + columns] = total.astype(BF16)
        column_sums = jnp.sum(total * total, axis=0, keepdims=True)
        square += jnp.sum(column_sums, axis=1, keepdims=True)
    square_out.ref[...] = jnp.broadcast_to(square.reshape(1, 1, 1), square_out.ref.shape)


def sum_parts(parts, first, count):
    return functools.reduce(jnp.add, [parts[first + at] for at in range(count)])


def square_body(numbers, arriving, leaving):
    total = sum_parts(arriving[0], 0, Z * CORE)
    leaving[0].ref[...] = jnp.broadcast_to(total[None], leaving[0].ref.shape)


def final_body(numbers, arriving, leaving):
    (core,) = numbers
    squares, near, far, noise_value, noise_out = arriving
    value, out = leaving
    columns = value.ref.shape[1]
    clip_bound = math.sqrt(2.0 * D * HEADS * HEAD_DIM)
    factors = []
    for image in range(YH):
        total = sum_parts(squares, image * 8, 8)[0:1, 0:1]
        factors.append(clip_bound / (jnp.sqrt(total) + 0.01))
    near_factor = jnp.where(core == 0, factors[0], factors[1])
    far_factor = jnp.where(core == 0, factors[1], factors[0])
    weighted = near_factor * near[...].astype(F32) + far_factor * far[...].astype(F32)
    value.ref[...] = (weighted[:, :columns] + noise_value[...]) * 0.5
    out.ref[...] = (weighted[:, columns:] + noise_out[...]) * 0.5


def local(tokens, w_query, w_key, w_value, w_out, cotangent, noise_value, noise_out):
    images, rows, width = tokens.shape
    columns = w_query.shape[1]
    heads = columns // HEAD_DIM
    image = lax.axis_index("yh")
    z = lax.axis_index("z")
    core = lax.axis_index("core")
    flat_tokens = tokens.reshape(images * rows, width)
    flat_cotangent = cotangent.reshape(images * rows, width)
    shape = jax.ShapeDtypeStruct
    here, this_core, this_image = z.reshape(1), core.reshape(1), image.reshape(1)

    def project(weight):
        return jnp.dot(flat_tokens, weight, preferred_element_type=F32).astype(BF16)

    def pick(array, index):
        return lax.dynamic_index_in_dim(array, index, 0, keepdims=False)

    def image_rows(array):
        array = array.reshape(images, rows, array.shape[1])
        partner = swap(pick(array, 1 - image), "yh", YH)
        return jnp.concatenate([pick(array, image), partner], axis=0)

    def from_partner(array):
        return lax.all_gather(pick(array, 1 - image), "yh", axis=0)

    keys_values = jnp.concatenate([project(w_key), project(w_value)], axis=1)
    chunk = image_rows(keys_values)
    d_attn = jnp.einsum("rd,cd->rc", flat_cotangent, w_out, preferred_element_type=F32)
    queries_d = jnp.concatenate([project(w_query), d_attn.astype(BF16)], axis=1)
    chunk, queries_d = lax.optimization_barrier((chunk, queries_d))
    queries_d = image_rows(queries_d)
    chip_rows = CORE * images * rows

    def stats_of(chosen, *carried):
        (found,) = call(
            functools.partial(stats_body, heads, len(chosen)),
            "stats",
            (),
            (queries_d, *chosen, *carried),
            (shape((8, chip_rows), F32),),
            {at: left_part(x) for at, x in enumerate((queries_d, *chosen))},
        )
        return found

    def left_part(x):
        return (x.shape[0], columns), lambda *_: (slice(None), slice(0, columns))

    def right_part(x):
        return (x.shape[0], columns), lambda *_: (slice(None), slice(columns, 2 * columns))

    forward = backward = chunk
    pieces = [chunk]
    for step in range(1, 4):
        forward = shift(forward, "z", Z, 1)
        backward = shift(backward, "z", Z, -1)
        pieces += [forward, backward]
        if step == 1:
            forward, backward, queries_d, late_cotangent = lax.optimization_barrier(
                (forward, backward, queries_d, cotangent)
            )
            queries_d = jnp.concatenate([queries_d, swap(queries_d, "core", CORE)], axis=0)
            cotangent_pair = cotangent, from_partner(late_cotangent)
        if step == 3:
            stats = stats_of(pieces[:3])
            forward, backward, stats = lax.optimization_barrier((forward, backward, stats))
    pieces.append(shift_by_core(jnp.where(core == 0, forward, backward), 1))
    stats = stats_of(pieces[3:7], stats)
    stats = stats_of(pieces[7:], stats)
    other_stats = swap(stats, "core", CORE)

    def block(parts, count):
        return shape((parts, count, columns), BF16)

    def start_scatter(near_f, near_b, far):
        return shift(near_f, "z", Z, 1), shift(near_b, "z", Z, -1), shift_by_core(far, 2)

    def relay(arrived, keep_f, keep_b):
        like = shape(keep_f.shape, BF16)
        return call(
            relay_body,
            "relay",
            (this_core,),
            (*arrived, keep_f, keep_b),
            (like, like),
            vmem=LARGE,
        )

    def end_scatter(arrived, sums, own):
        return own, arrived[0], arrived[1], shift(sums[0], "z", Z, 2), shift(sums[1], "z", Z, -2)

    distances = (0, 1, 7, 2, 6, 3, 5, 4)
    d_value, attended = call(
        functools.partial(d_value_body, heads, distances),
        "d_value",
        (here,),
        (queries_d, queries_d, stats, other_stats, *pieces),
        (block(Z, 2 * rows), shape((2, columns, chip_rows // 2), BF16)),
        {0: left_part(queries_d), 1: right_part(queries_d)},
        LARGE,
    )
    attended, cotangent_pair, late_tokens = lax.optimization_barrier(
        (attended, cotangent_pair, tokens)
    )
    tokens_pair = tokens, swap(pick(late_tokens, 1 - image), "yh", YH)[None]
    terms = lax.all_to_all(d_value, "z", 0, 0, tiled=True)
    attended_other = swap(attended, "core", CORE)

    def half_width(pair):
        turned = shape((width // 2, 2 * rows), BF16)
        keep, send = call(
            turn_body,
            "turn",
            (this_core, this_image),
            pair,
            (turned, turned),
            {
                0: ((rows, width), lambda core, image: image),
                1: ((rows, width), lambda core, image: (pair[1].shape[0] - 1) * (1 - image)),
            },
            LARGE,
        )
        return keep, swap(send, "core", CORE)

    cotangent_half = half_width(cotangent_pair)
    (per_out,) = call(
        out_grad_body,
        "per_out",
        (),
        (*cotangent_half, attended, attended_other),
        (shape((width // 2, columns), BF16),),
        vmem=LARGE,
    )
    out_shard = lax.psum_scatter(per_out, "z", scatter_dimension=0, tiled=True)
    tokens_half = half_width(tokens_pair)

    (d_value,) = call(sum_body, "d_value_sum", (), (terms,), (shape((2 * rows, columns), BF16),))
    count = width // 2 // Z
    parts = call(
        value_grad_body,
        "per_value",
        (here,),
        (*tokens_half, d_value, swap(d_value, "core", CORE)),
        (block(2, count), block(2, count)) + (block(1, count),) * 4,
        vmem=LARGE,
    )
    arrived = start_scatter(*parts[:3])
    terms = end_scatter(arrived, relay(arrived, *parts[3:5]), parts[5])
    small = shape((Z * CORE, 8, 128), F32)
    shard, square = call(
        shard_body,
        "shards",
        (),
        (out_shard, *terms),
        (shape((count, 2 * columns), BF16), small),
        vmem=LARGE,
    )

    halves = shard.reshape(2, count // 2, 2 * columns)
    pairs = ([(0, 0), (1, 2), (2, 1), (3, 3)], [(0, 1), (1, 3), (2, 0), (3, 2)])
    along = [
        [((s // 2 * Z + k) * 2 + s % 2, (t // 2 * Z + k) * 2 + t % 2) for k in range(Z) for s, t in pair]
        for pair in pairs
    ]
    axes = ("yh", "z", "core")
    near = lax.ppermute(pick(halves, image), axes, along[0])
    far = lax.ppermute(pick(halves, 1 - image), axes, along[1])

    squares = lax.all_to_all(square, ("z", "core"), 0, 0, tiled=True)
    (squares,) = call(square_body, "squares", (), (squares,), (small,))
    squares = lax.all_to_all(squares, ("yh", "yl", "x"), 0, 0, tiled=True)
    rows_of_both = shape(noise_value.shape, F32)
    grad_value, grad_out = call(
        final_body,
        "final",
        (this_core,),
        (squares, near, far, noise_value, noise_out.T),
        (rows_of_both, rows_of_both),
    )
    return grad_value, grad_out.T


def solution(mesh):
    fine = Mesh(mesh.devices.reshape(YH, Z, CORE, 2, 4), ("yh", "z", "core", "yl", "x"))
    seq, tensor = ("yh", "z", "core"), ("yl", "x")
    placed = (
        P(None, seq, None),
        P(None, tensor),
        P(None, tensor),
        P(None, tensor),
        P(tensor, None),
        P(None, seq, None),
        P(seq, tensor),
        P(tensor, seq),
    )
    return jax.shard_map(
        local,
        mesh=fine,
        in_specs=placed,
        out_specs=(P(seq, tensor), P(tensor, seq)),
        check_vma=False,
    )
```
